32 devices in a mesh: group: 4 (over y, core), member: 8 (over z, x).
Axes of the slice: x: 2, y: 2, z: 4, core: 2. Of those that a mesh axis runs over, the one named last changes fastest.
Arguments:
- store: float32 [32768, 1024], P(('group', 'member')), may hold values from -6 to 6
- cache: float32 [4096, 1024], P('member'), may hold values from -6 to 6
- hot_local: int32 [32, 1], P(('group', 'member')), may hold values from 0 to 7
- hit_member: int32 [32768, 1], P(('group', 'member')), may hold values from 0 to 7; in each aligned block of 1024 rows (0 to 1023, 1024 to 2047, ...) at most 256 rows name the same one
- hit_row: int32 [32768], P(('group', 'member')), may hold values from 0 to 511
- miss_owner: int32 [16384, 1], P(('group', 'member')), may hold values from 0 to 31; in each aligned block of 512 rows (0 to 511, 512 to 1023, ...) at most 32 rows name the same one
- miss_row: int32 [16384], P(('group', 'member')), may hold values from 0 to 1023
- tgt_self: int32 [32768], P(('group', 'member')), may hold values from 0 to 1535
- tgt_nbr: int32 [32768, 10], P(('group', 'member')), may hold values from 0 to 1535
- tgt_mask: int32 [32768, 10], P(('group', 'member')), may hold values 0 or 1
- seed_self: int32 [4096], P(('group', 'member')), may hold values from 0 to 1023
- seed_nbr: int32 [4096, 5], P(('group', 'member')), may hold values from 0 to 1023
- seed_mask: int32 [4096, 5], P(('group', 'member')), may hold values 0 or 1
- w1_self: bfloat16 [1024, 512], replicated, may hold values from -0.1875 to 0.1875
- w1_nbr: bfloat16 [1024, 512], replicated, may hold values from -0.1875 to 0.1875
- w2_self: bfloat16 [512, 512], replicated, may hold values from -0.25 to 0.25
- w2_nbr: bfloat16 [512, 512], replicated, may hold values from -0.25 to 0.25
- d_emb: bfloat16 [4096, 512], P(('group', 'member')), may hold values from -6 to 6
Outputs:
- emb: bfloat16 [4096, 512], P(('group', 'member'))
- grad_w1_self: float32 [1024, 512], replicated
- grad_w1_nbr: float32 [1024, 512], replicated
- grad_w2_self: float32 [512, 512], replicated
- grad_w2_nbr: float32 [512, 512], replicated
- new_cache: float32 [4096, 1024], P('member')
The draws below stay inside these ranges and needn't reach their ends.
Inputs may be any that keep to these rules, and one draw needn't show every extreme that they name: `hit_member`: among the rows of one device at most 256 name the same member, a bound that some block reaches of them. `miss_owner`: among the rows of one device at most 32 name the same owner, a bound that some block reaches of them.
All inputs are finite; a program needn't handle non-finite values. No bound on the sum of `tgt_mask` or of `seed_mask` on one device may be relied on, other than what follows from the above.
Results may differ from the reference program's by a relative error of at most 0.0067.
Values may be sent and summed in bfloat16 or wider, within the bound.
No kernel may reach another device: no remote copies, remote signals or barrier semaphores. Data moves between devices by JAX's collectives and lax.ppermute only.
A program may use at most 128 MiB of HBM per device.

```python
import math
import jax
import jax.numpy as jnp
import numpy as np
from jax import lax

W = 1024
H = 512
BLOCK = 128
FAN1 = 10
FAN2 = 5
HOT_OWN = 1
BLK_DEV = 8
HIT_DEV = 1024
MISS_DEV = 512
TGT_DEV = 1024
SEED_DEV = 128
CAP_H = 256
CAP_M = 32
CACHE_DEV = 512
CACHE_ROWS = 4096
STORE_ROWS = 32768
HITS = 32768
MISSES = 16384
TGTS = 32768
SEEDS = 4096
N_GROUP = 4
N_MEMBER = 8
DEVICES = 32


def with_ends(drawn, rng, smallest, top_value):
    index_at = [jax.random.randint(jax.random.fold_in(rng, axis), (), 0, length) for axis, length in enumerate(drawn.shape)]
    widest = drawn.shape.index(max(drawn.shape))
    beside = index_at[:widest] + [(index_at[widest] + 1) % drawn.shape[widest]] + index_at[widest + 1:]
    return drawn.at[tuple(index_at)].set(smallest).at[tuple(beside)].set(top_value)


def block_levels(rng, shape, cuts, smallest, largest):
    level, own = 1.0, jax.random.fold_in(rng, 6)
    for axis_at, shards_of in cuts:
        heights = jnp.exp(jax.random.uniform(jax.random.fold_in(own, axis_at), (shards_of,), jnp.float32, smallest / len(cuts), largest / len(cuts)))
        level = level * jnp.repeat(heights, shape[axis_at] // shards_of).reshape([-1 if axis == axis_at else 1 for axis in range(len(shape))])
    return level


def routed_block(rng, own, number, rows, count, top, most, lean):
    ranking = jax.random.permutation(rng, count)
    heavy_load, ordinary = portions_of(count, rows * top, most, lean, True), portions_of(count, rows * top, most, lean, False)
    places = jnp.arange(count)

    def named(tallies, rotation):
        used = int((tallies > 0).sum())
        fixed = max(1, used // 4)
        passed = fixed + (places - fixed + rotation * (used - fixed)) % max(1, count - fixed)
        return jnp.zeros((count,), jnp.int32).at[ranking[jnp.where(places < fixed, places, passed)]].set(jnp.asarray(tallies, jnp.int32))

    tallies = jnp.where(number % 4 == 0, named(heavy_load, number // 4), named(ordinary, number - number // 4 - 1))
    mixed = jax.random.permutation(jax.random.fold_in(own, 3), count)
    donor, receiver = mixed[0:count // 2 * 2:2], mixed[1:count // 2 * 2:2]
    room = jnp.minimum(tallies[donor] - 1, most - tallies[receiver]) // 2
    room = jnp.where((donor == ranking[0]) | (receiver == ranking[0]) | (tallies[receiver] == 0), 0, jnp.maximum(room, 0))
    passed = jax.random.randint(jax.random.fold_in(own, 4), (count // 2,), 0, 1 << 20) % (room + 1)
    tallies = tallies.at[donor].add(-passed).at[receiver].add(passed)
    items = jnp.searchsorted(jnp.cumsum(tallies), jnp.arange(rows * top), side="right").astype(jnp.int32)
    table = items.reshape(top, rows).T
    table = table[jax.random.permutation(jax.random.fold_in(own, 1), rows)]
    rotation = jax.random.randint(jax.random.fold_in(own, 2), (rows, 1), 0, top)
    return jnp.take_along_axis(table, (jnp.arange(top)[None, :] + rotation) % top, axis=1)


def portions_of(number_of, total, limit, slope, full):
    weights = [(1 << 20) // math.isqrt(grade ** slope) + 1 for grade in range(1, number_of + 1)]
    largest = limit if full else min(limit, max(-(-total // number_of), total * weights[0] // sum(weights)))
    least = 1 if total - largest >= number_of - 1 else 0
    holding, rest = [largest] + [least] * (number_of - 1), total - largest - least * (number_of - 1)
    while rest > 0:
        free = [i for i in range(1, number_of) if holding[i] < largest] or [i for i in range(1, number_of) if holding[i] < limit]
        pool, left = sum([weights[i] for i in free]), rest
        for i in free:
            addition = min(limit - holding[i], max(1, left * weights[i] // pool), rest)
            holding[i] = holding[i] + addition
            rest = rest - addition
    return np.array(holding)


def centred(key, extent, width, bound, split=(), held_as=jnp.bfloat16):
    entries = jax.random.normal(key, extent, jnp.float32) * width
    if len(split) > 0:
        entries = block_levels(key, extent, split, -0.22, 0.18) * entries
    return jnp.clip(entries, min=-bound, max=bound).astype(held_as)


def setup_inputs(seed: int = 0) -> dict:
    arg_keys = jax.random.split(jax.random.key(seed), 19)
    store = centred(arg_keys[0], (STORE_ROWS, W), 1.0, 6.0, ((0, 32),), jnp.float32)
    cache = centred(arg_keys[1], (CACHE_ROWS, W), 1.0, 6.0, ((0, 8),), jnp.float32)
    hot_local = with_ends(jax.random.randint(arg_keys[2], (DEVICES, HOT_OWN), 0, BLK_DEV), jax.random.fold_in(arg_keys[2], 1), 0, BLK_DEV - 1).astype(jnp.int32)
    hit_member_keys = jax.random.split(jax.random.fold_in(arg_keys[3], 1), HITS // HIT_DEV)
    hit_member_turns = jax.random.permutation(jax.random.fold_in(arg_keys[3], 3), HITS // HIT_DEV)
    hit_member = jax.vmap(lambda own, number: routed_block(jax.random.fold_in(arg_keys[3], 2), own, number, HIT_DEV, N_MEMBER, 1, CAP_H, 1))(hit_member_keys, hit_member_turns).reshape((HITS, 1))
    hit_row = with_ends(jax.random.randint(arg_keys[4], (HITS,), 0, CACHE_DEV), jax.random.fold_in(arg_keys[4], 1), 0, CACHE_DEV - 1).astype(jnp.int32)
    miss_owner_keys = jax.random.split(jax.random.fold_in(arg_keys[5], 1), MISSES // MISS_DEV)
    miss_owner_turns = jax.random.permutation(jax.random.fold_in(arg_keys[5], 3), MISSES // MISS_DEV)
    miss_owner = jax.vmap(lambda own, number: routed_block(jax.random.fold_in(arg_keys[5], 2), own, number, MISS_DEV, DEVICES, 1, CAP_M, 2))(miss_owner_keys, miss_owner_turns).reshape((MISSES, 1))
    miss_row = with_ends(jax.random.randint(arg_keys[6], (MISSES,), 0, BLK_DEV * BLOCK), jax.random.fold_in(arg_keys[6], 1), 0, (BLK_DEV * BLOCK) - 1).astype(jnp.int32)
    tgt_self = with_ends(jax.random.randint(arg_keys[7], (TGTS,), 0, HIT_DEV + MISS_DEV), jax.random.fold_in(arg_keys[7], 1), 0, (HIT_DEV + MISS_DEV) - 1).astype(jnp.int32)
    tgt_nbr = with_ends(jax.random.randint(arg_keys[8], (TGTS, FAN1), 0, HIT_DEV + MISS_DEV), jax.random.fold_in(arg_keys[8], 1), 0, (HIT_DEV + MISS_DEV) - 1).astype(jnp.int32)
    tgt_mask = with_ends((jax.random.randint(arg_keys[9], (TGTS, FAN1), 0, 2) < 1).astype(jnp.int32), jax.random.fold_in(arg_keys[9], 1), 0, 1)
    seed_self = with_ends(jax.random.randint(arg_keys[10], (SEEDS,), 0, TGT_DEV), jax.random.fold_in(arg_keys[10], 1), 0, TGT_DEV - 1).astype(jnp.int32)
    seed_nbr = with_ends(jax.random.randint(arg_keys[11], (SEEDS, FAN2), 0, TGT_DEV), jax.random.fold_in(arg_keys[11], 1), 0, TGT_DEV - 1).astype(jnp.int32)
    seed_mask = with_ends((jax.random.randint(arg_keys[12], (SEEDS, FAN2), 0, 2) < 1).astype(jnp.int32), jax.random.fold_in(arg_keys[12], 1), 0, 1)
    w1_self = centred(arg_keys[13], (W, H), W ** -0.5, 0.1875)
    w1_nbr = centred(arg_keys[14], (W, H), W ** -0.5, 0.1875)
    w2_self = centred(arg_keys[15], (H, H), H ** -0.5, 0.25)
    w2_nbr = centred(arg_keys[16], (H, H), H ** -0.5, 0.25)
    d_emb = centred(arg_keys[17], (SEEDS, H), 1.0, 6.0, ((0, 32),))
    return dict(store=store, cache=cache, hot_local=hot_local, hit_member=hit_member, hit_row=hit_row, miss_owner=miss_owner, miss_row=miss_row, tgt_self=tgt_self, tgt_nbr=tgt_nbr, tgt_mask=tgt_mask, seed_self=seed_self, seed_nbr=seed_nbr, seed_mask=seed_mask, w1_self=w1_self, w1_nbr=w1_nbr, w2_self=w2_self, w2_nbr=w2_nbr, d_emb=d_emb)


def silu_slope(pre):
    gate_sig = jax.nn.sigmoid(pre)
    return gate_sig * (1.0 + pre * (1.0 - gate_sig))

def reference(store, cache, hot_local, hit_member, hit_row, miss_owner, miss_row, tgt_self, tgt_nbr, tgt_mask, seed_self, seed_nbr, seed_mask, w1_self, w1_nbr, w2_self, w2_nbr, d_emb):
    feat_width = store.shape[1]
    blocks = store.reshape(DEVICES, BLK_DEV, BLOCK, feat_width)
    chosen = jax.vmap(lambda owned, picks: owned[picks])(blocks, hot_local)
    new_cache = chosen.reshape(N_GROUP, N_MEMBER, HOT_OWN * BLOCK, feat_width).transpose(1, 0, 2, 3).reshape(-1, feat_width)
    hit_index = (hit_member[:, 0] * CACHE_DEV + hit_row).astype(jnp.int32)
    hit_feats = cache[hit_index].astype(jnp.bfloat16).reshape(DEVICES, HIT_DEV, feat_width)
    miss_index = (miss_owner[:, 0] * (BLK_DEV * BLOCK) + miss_row).astype(jnp.int32)
    miss_feats = store[miss_index].astype(jnp.bfloat16).reshape(DEVICES, MISS_DEV, feat_width)

    def device_step(carry, items):
        hit_part, miss_part, target_self, target_nbr, target_mask, own_seed, seed_list, seed_flags, cotan = items
        fetched = jnp.concatenate([hit_part, miss_part], 0)
        mask_one = target_mask.astype(jnp.float32)
        count_one = jnp.maximum(lax.optimization_barrier(jnp.sum(mask_one, 1)), 1.0)
        gathered = fetched[target_nbr].astype(jnp.float32) * mask_one[:, :, None]
        mean_one = (lax.optimization_barrier(jnp.sum(gathered, 1)) / count_one[:, None]).astype(jnp.bfloat16)
        self_one = fetched[target_self]
        pre_one = jnp.dot(self_one, w1_self, preferred_element_type=jnp.float32) + jnp.dot(mean_one, w1_nbr, preferred_element_type=jnp.float32)
        hidden = jax.nn.silu(pre_one).astype(jnp.bfloat16)
        mask_two = seed_flags.astype(jnp.float32)
        count_two = jnp.maximum(lax.optimization_barrier(jnp.sum(mask_two, 1)), 1.0)
        gathered_two = hidden[seed_list].astype(jnp.float32) * mask_two[:, :, None]
        mean_two = (lax.optimization_barrier(jnp.sum(gathered_two, 1)) / count_two[:, None]).astype(jnp.bfloat16)
        self_two = hidden[own_seed]
        embedded = (jnp.dot(self_two, w2_self, preferred_element_type=jnp.float32) + jnp.dot(mean_two, w2_nbr, preferred_element_type=jnp.float32)).astype(jnp.bfloat16)
        term_w2_self = jnp.dot(self_two.T, cotan, preferred_element_type=jnp.float32)
        term_w2_nbr = jnp.dot(mean_two.T, cotan, preferred_element_type=jnp.float32)
        back_self = jnp.dot(cotan, w2_self.T, preferred_element_type=jnp.float32).astype(jnp.bfloat16)
        back_mean = (jnp.dot(cotan, w2_nbr.T, preferred_element_type=jnp.float32) / count_two[:, None]).astype(jnp.bfloat16)
        back_hidden = jnp.zeros((TGT_DEV, H), jnp.float32).at[own_seed].add(back_self.astype(jnp.float32))
        spread = (mask_two[:, :, None] * back_mean[:, None, :].astype(jnp.float32)).reshape(-1, H)
        back_hidden = back_hidden.at[seed_list.reshape(-1)].add(spread)
        back_pre = (back_hidden * silu_slope(pre_one)).astype(jnp.bfloat16)
        term_w1_self = jnp.dot(self_one.T, back_pre, preferred_element_type=jnp.float32)
        term_w1_nbr = jnp.dot(mean_one.T, back_pre, preferred_element_type=jnp.float32)
        updated = (carry[0] + term_w1_self, carry[1] + term_w1_nbr, carry[2] + term_w2_self, carry[3] + term_w2_nbr)
        return (updated, embedded)
    start = (jnp.zeros((feat_width, H), jnp.float32), jnp.zeros((feat_width, H), jnp.float32), jnp.zeros((H, H), jnp.float32), jnp.zeros((H, H), jnp.float32))
    items = (hit_feats, miss_feats, tgt_self.reshape(DEVICES, TGT_DEV), tgt_nbr.reshape(DEVICES, TGT_DEV, FAN1), tgt_mask.reshape(DEVICES, TGT_DEV, FAN1), seed_self.reshape(DEVICES, SEED_DEV), seed_nbr.reshape(DEVICES, SEED_DEV, FAN2), seed_mask.reshape(DEVICES, SEED_DEV, FAN2), d_emb.reshape(DEVICES, SEED_DEV, H))
    totals, embedded = lax.scan(device_step, start, items)
    grad_scale = 1.0 / math.sqrt(SEEDS)
    return (embedded.reshape(-1, H), totals[0] * grad_scale, totals[1] * grad_scale, totals[2] * grad_scale, totals[3] * grad_scale, new_cache)
```

```python
import functools
import math

import jax
import jax.numpy as jnp
from jax import lax
from jax.experimental import pallas as pl
from jax.experimental.pallas import tpu as pltpu
from jax.sharding import PartitionSpec as P

BLOCK = 128
BOTH = ("group", "member")
F32, BF16, I32 = jnp.float32, jnp.bfloat16, jnp.int32
GRANT = 29 * 1024 * 1024


def dot(a, b, ca=1, cb=0):
    return lax.dot_general(a, b, (((ca,), (cb,)), ((), ())), preferred_element_type=F32)


def iota(shape, dim):
    return lax.broadcasted_iota(I32, shape, dim)


def kernel_call(body, out_shape, scratch=(), smem=0, flops=0):
    def call(*operands):
        specs = [pl.BlockSpec(memory_space=pltpu.SMEM)] * smem
        specs += [pl.BlockSpec(memory_space=pltpu.VMEM)] * (len(operands) - smem)
        return pl.pallas_call(
            body,
            out_shape=out_shape,
            in_specs=specs,
            out_specs=jax.tree.map(lambda _: pl.BlockSpec(memory_space=pltpu.VMEM), out_shape),
            scratch_shapes=list(scratch),
            compiler_params=pltpu.CompilerParams(vmem_limit_bytes=GRANT),
            cost_estimate=pl.CostEstimate(flops=0, bytes_accessed=0, transcendentals=0),
        )(*operands)

    return call


def request_body(owner_ref, row_ref, ids_ref, slot_ref):
    count = owner_ref.shape[1]
    owners, cap = ids_ref.shape
    flags = owner_ref[...] == iota((owners, count), 0)
    flag = flags.astype(F32).astype(BF16)
    earlier = (iota((count, count), 0) < iota((count, count), 1)).astype(F32).astype(BF16)
    rank = jnp.sum(jnp.where(flags, dot(flag, earlier), 0.0), axis=0, keepdims=True).astype(I32)
    slot_ref[...] = owner_ref[...] * cap + rank
    ranked = (rank == iota((cap, count), 0)).astype(F32).astype(BF16)
    row = row_ref[...]
    high = jnp.where(flags, (row // 128).astype(F32), 0.0).astype(BF16)
    low = jnp.where(flags, (row % 128).astype(F32), 0.0).astype(BF16)
    ids_ref[...] = (dot(high, ranked, 1, 1) * 128.0 + dot(low, ranked, 1, 1)).astype(I32)


def serve_body(ids_ref, store_ref, rows_ref):
    peers, cap = ids_ref.shape
    total, held = peers * cap, store_ref.shape[0]
    ids = ids_ref[...]
    spread = (iota((total, peers), 0) // cap == iota((total, peers), 1)).astype(F32).astype(BF16)
    high = dot(spread, (ids // 128).astype(F32).astype(BF16))
    low = dot(spread, (ids % 128).astype(F32).astype(BF16))
    here = iota((total, cap), 0) % cap == iota((total, cap), 1)
    flat = jnp.sum(jnp.where(here, high * 128.0 + low, 0.0), axis=1, keepdims=True).astype(I32)
    step = 256
    for at in range(0, total, step):
        pick = (flat[at : at + step] == iota((step, held), 1)).astype(F32).astype(BF16)
        rows_ref[at : at + step, :] = dot(pick, store_ref[...]).astype(BF16)


def tables_body(
    targets_ref, names_ref, slot_ref, mask_ref, code_ref, emb_ref, w2s_ref, w2n_ref,
    sel_hit_ref, sel_miss_ref, count_ref, back_ref, flag_ref, column_ref, *, hits,
):
    seeds, total = targets_ref.shape[1], names_ref.shape[1]
    misses = slot_ref.shape[1]
    slots = sel_miss_ref.shape[2]
    fan, fan_two = names_ref.shape[0] - 1, mask_ref.shape[0]

    def columns(rows):
        rows = rows.astype(F32)
        pad = jnp.zeros((-rows.shape[0] % 8, rows.shape[1]), F32)
        return jnp.concatenate([rows, pad], 0).T if pad.shape[0] else rows.T

    column_ref[...] = columns(code_ref[...])[:, 0:1].astype(I32)
    names = names_ref[...]
    high = (names // 128).astype(F32).astype(BF16)
    low = (names % 128).astype(F32).astype(BF16)
    place = (slot_ref[...] == iota((slots, misses), 0)).astype(F32).astype(BF16)
    targets = columns(targets_ref[...]).astype(I32)
    for turn in range(fan_two + 1):
        cut = slice(turn * seeds, (turn + 1) * seeds)
        pick = (targets[:, turn : turn + 1] == iota((seeds, total), 1)).astype(F32).astype(BF16)
        named = (dot(pick, high, 1, 1) * 128.0 + dot(pick, low, 1, 1)).astype(I32) - 1
        here = named[:, 1:] >= 0
        count_ref[cut, :] = jnp.maximum(jnp.sum(here.astype(F32), axis=1, keepdims=True), 1.0)
        for first, width in ((0, hits), (hits, misses)):
            lane = iota((seeds, width), 1) + first
            own = jnp.where(named[:, 0:1] == lane, 1.0, 0.0).astype(BF16)
            near = jnp.zeros((seeds, width), F32)
            for k in range(1, fan + 1):
                near = near + jnp.where(named[:, k : k + 1] == lane, 1.0, 0.0)
            near = near.astype(BF16)
            if first == 0:
                sel_hit_ref[0, cut, :] = own
                sel_hit_ref[1, cut, :] = near
            else:
                sel_miss_ref[0, cut, :] = dot(own, place, 1, 1).astype(BF16)
                sel_miss_ref[1, cut, :] = dot(near, place, 1, 1).astype(BF16)
    mask = columns(mask_ref[...])[:, :fan_two]
    flag_ref[...] = mask
    count_two = jnp.maximum(jnp.sum(mask, axis=1, keepdims=True), 1.0)
    back_ref[0:seeds, :] = dot(emb_ref[...], w2s_ref[...], 1, 1).astype(BF16)
    back_mean = (dot(emb_ref[...], w2n_ref[...], 1, 1) / count_two).astype(BF16).astype(F32)
    for k in range(fan_two):
        at = (k + 1) * seeds
        back_ref[at : at + seeds, :] = (mask[:, k : k + 1] * back_mean).astype(BF16)


def cached_body(code_ref, *refs, bases):
    pieces, held_ref = refs[:-1], refs[-1]
    step = 256

    @pl.loop(0, code_ref.shape[0] // step)
    def _(turn):
        cut = pl.ds(pl.multiple_of(turn * step, step), step)
        total = None
        for piece, base in zip(pieces, bases):
            lane = iota((step, piece.shape[0]), 1) + base
            pick = (code_ref[cut, :] == lane).astype(F32).astype(BF16)
            part = dot(pick, piece[...])
            total = part if total is None else total + part
        held_ref[cut, :] = total.astype(BF16)


def share_body(sel_ref, *refs):
    parts, (own_ref, near_ref) = refs[:-2], refs[-2:]
    held = parts[0][...]
    for part in parts[1:]:
        held = held + part[...]
    step = 256
    for at in range(0, own_ref.shape[0], step):
        own_ref[at : at + step, :] = dot(sel_ref[0, at : at + step, :], held).astype(BF16)
        near_ref[at : at + step, :] = dot(sel_ref[1, at : at + step, :], held)


def join_body(me_ref, *refs, count, parts):
    pieces, outs = refs[:count], refs[count:]
    for k in range(count):
        depth = pieces[k].shape[0] // parts
        place = pl.multiple_of((me_ref[0] ^ k) * depth, 16)
        for j in range(parts):
            value = pieces[k][j * depth : (j + 1) * depth, :]
            outs[j][pl.ds(place, depth), :] = value.astype(outs[j].dtype)


def join(pieces, me, dtype, parts=1):
    count = len(pieces)
    depth, width = pieces[0].shape[0] // parts, pieces[0].shape[1]
    if depth % 16 == 0:
        return kernel_call(
            functools.partial(join_body, count=count, parts=parts),
            [jax.ShapeDtypeStruct((count * depth, width), dtype)] * parts,
            smem=1,
        )(me.reshape(1), *pieces)
    outs = [jnp.zeros((count * depth, width), dtype)] * parts
    for k in range(count):
        for j in range(parts):
            value = pieces[k][j * depth : (j + 1) * depth].astype(dtype)
            outs[j] = lax.dynamic_update_slice_in_dim(outs[j], value, (me ^ k) * depth, 0)
    return outs


def step_body(core_ref, *refs, scale, step):
    sources, (count_ref, mask_ref, out_ref, send_ref, keep_ref, *refs) = refs[:10], refs[10:]
    held, (self_ref, mean_ref, hid_ref, bp_ref, sems) = refs[:10], refs[10:]
    miss_ref, w1s_ref, w1n_ref, back_ref, w2s_ref, w2n_ref, emb_ref, *turned = held
    sel_ref, own_ref, near_ref = turned
    rows, wide = own_ref.shape
    seeds = mask_ref.shape[0]
    hid = w1s_ref.shape[1]
    turns = rows // step

    def copy(i, turn=None):
        source, target, number = sources[i], held[i], i
        if turn is not None:
            cut = slice(turn * step, (turn + 1) * step)
            source, target = (
                (ref.at[:, cut, :] if len(ref.shape) == 3 else ref.at[cut, :])
                for ref in (source, target)
            )
            number = 7 + (i - 7) * turns + turn
        return pltpu.make_async_copy(source, target, sems.at[number])

    order = [(0,), (7, 0), (8, 0), (9, 0), (1,), (2,), (3,)]
    order += [(i, turn) for turn in range(1, turns) for i in (7, 8, 9)] + [(4,), (5,), (6,)]
    for item in order:
        copy(*item).start()
    copy(0).wait()
    for turn in range(turns):
        cut = slice(turn * step, (turn + 1) * step)
        copy(7, turn).wait()
        own = dot(sel_ref[0, cut, :], miss_ref[...])
        near = dot(sel_ref[1, cut, :], miss_ref[...])
        copy(8, turn).wait()
        copy(9, turn).wait()
        own = (own_ref[cut, :].astype(F32) + own).astype(BF16)
        mean = ((near_ref[cut, :] + near) / count_ref[cut, :]).astype(BF16)
        self_ref[cut, :] = own
        mean_ref[cut, :] = mean
        if turn == 0:
            copy(1).wait()
            copy(2).wait()
        pre = dot(own, w1s_ref[...]) + dot(mean, w1n_ref[...])
        gate = jax.nn.sigmoid(pre)
        hid_ref[cut, :] = (pre * gate).astype(BF16)
        slope = gate * (1.0 + pre * (1.0 - gate))
        if turn == 0:
            copy(3).wait()
        bp_ref[cut, :] = (back_ref[cut, :].astype(F32) * slope).astype(BF16)

    core = core_ref[0]
    half = (2 * wide + 2 * hid) // 2

    def put(at, value):
        value = value * scale
        place = slice(at % half, at % half + value.shape[0])

        @pl.when(core == at // half)
        def _():
            keep_ref[place, :] = value

        @pl.when(core != at // half)
        def _():
            send_ref[place, :] = value.astype(BF16)

    mask = mask_ref[...]
    count_two = jnp.maximum(jnp.sum(mask, axis=1, keepdims=True), 1.0)
    total = jnp.zeros((seeds, hid), F32)
    for k in range(mask.shape[1]):
        at = (k + 1) * seeds
        total = total + mask[:, k : k + 1] * hid_ref[at : at + seeds, :].astype(F32)
    mean_two = (total / count_two).astype(BF16)
    self_two = hid_ref[0:seeds, :]
    for i in (4, 5, 6):
        copy(i).wait()
    out_ref[...] = (dot(self_two, w2s_ref[...]) + dot(mean_two, w2n_ref[...])).astype(BF16)
    put(2 * wide, dot(self_two, emb_ref[...], 0, 0))
    put(2 * wide + hid, dot(mean_two, emb_ref[...], 0, 0))
    for base, ref in ((0, self_ref), (wide, mean_ref)):
        for at in range(0, wide, step):
            put(base + at, dot(ref[:, at : at + step], bp_ref[...], 0, 0))


def finish_body(core_ref, *refs, cuts):
    (p, p_far, q, q_far), outs, held, sems = refs[:4], refs[4:8], refs[8:12], refs[12]
    quarter = p.shape[0]
    for near_core in range(2):

        @pl.when(core_ref[0] == near_core)
        def _():
            order = [(p, p_far), (q, q_far)]
            order = [pair[core != near_core] for core in range(2) for pair in order]
            for i, (first, last) in enumerate(cuts):
                at = first
                while at < last:
                    number, place = at // quarter, at % quarter
                    upto = min(last, (number + 1) * quarter)
                    held[i][at - first : upto - first, :] = order[number][
                        place : place + upto - at, :
                    ].astype(F32)
                    at = upto
                pltpu.make_async_copy(held[i], outs[i], sems.at[i]).start()

    for i in range(len(cuts)):
        pltpu.make_async_copy(held[i], outs[i], sems.at[i]).wait()


class Slice:
    def __init__(self):
        self.groups, self.members = lax.axis_size("group"), lax.axis_size("member")
        self.size = {"c": 2, "y": self.groups // 2, "z": 4, "x": self.members // 4}
        group, member = lax.axis_index("group"), lax.axis_index("member")
        self.at = {
            "c": group % 2,
            "y": group // 2,
            "z": member // self.size["x"],
            "x": member % self.size["x"],
        }

    def swap(self, array, axis, k):
        stride = {"c": 1, "y": 2, "z": self.size["x"], "x": 1}[axis]
        name, count = ("group", self.groups) if axis in "cy" else ("member", self.members)
        return lax.ppermute(array, name, [(i, i ^ (k * stride)) for i in range(count)])

    def part(self, terms, axis, k):
        depth = terms[0].shape[0] // self.size[axis]
        place = (self.at[axis] ^ k) * depth
        return [lax.dynamic_slice_in_dim(term, place, depth, 0) for term in terms]

    def scatter(self, terms, axis):
        others = range(1, self.size[axis])
        got = [self.swap(total(self.part(terms, axis, k)).astype(BF16), axis, k) for k in others]
        return self.part(terms, axis, 0) + got

    def gather(self, part, axis, dtype=BF16, parts=1):
        pieces = [part] + [self.swap(part, axis, k) for k in range(1, self.size[axis])]
        return join(pieces, self.at[axis], dtype, parts)


def total(terms):
    out = terms[0].astype(F32)
    for term in terms[1:]:
        out = out + term.astype(F32)
    return out


def on_device(
    store,
    cache,
    hot_local,
    hit_member,
    hit_row,
    miss_owner,
    miss_row,
    tgt_self,
    tgt_nbr,
    tgt_mask,
    seed_self,
    seed_nbr,
    seed_mask,
    w1_self,
    w1_nbr,
    w2_self,
    w2_nbr,
    d_emb,
):
    box = Slice()
    nx, ny, nz = box.size["x"], box.size["y"], box.size["z"]
    wide, hid = w1_self.shape
    owners = box.groups * box.members
    hits, misses = hit_row.shape[0], miss_row.shape[0]
    cap = 2 * misses // owners
    seeds, fan_two = seed_nbr.shape
    rows = seeds * (fan_two + 1)

    share = cache.shape[0] // box.groups
    group = lax.axis_index("group")
    mine = lax.dynamic_slice_in_dim(cache, group * share, share, 0).astype(BF16)

    ids, slot = kernel_call(
        request_body,
        (
            jax.ShapeDtypeStruct((owners, cap), I32),
            jax.ShapeDtypeStruct((1, misses), I32),
        ),
        flops=2 * misses * misses * 128,
    )(miss_owner.reshape(1, -1), miss_row.reshape(1, -1))
    store_low = store.astype(BF16)
    asked = lax.all_to_all(
        ids.reshape(owners, 1, cap), BOTH, split_axis=0, concat_axis=0, tiled=True
    ).reshape(owners, cap)
    near = [mine] + [box.swap(mine, "z", k) for k in range(1, nz // 2)]

    targets = jnp.concatenate([seed_self[None, :], seed_nbr.T], 0)
    names = jnp.concatenate([tgt_self[None, :] + 1, jnp.where(tgt_mask > 0, tgt_nbr + 1, 0).T], 0)
    member, line = hit_member.reshape(1, -1), hit_row.reshape(1, -1)
    holder = line // share
    code = ((holder % 2) ^ box.at["c"]) * ny + ((holder // 2) ^ box.at["y"])
    code = code * nx + ((member % nx) ^ box.at["x"])
    code = code * nz + ((member // nx) ^ box.at["z"])
    code = code * share + line % share
    hot = lax.dynamic_slice_in_dim(store, hot_local[0, 0] * BLOCK, BLOCK, 0).astype(BF16)

    def side(part):
        found = {(k, 0): box.swap(part, "x", k) for k in range(1, nx)}
        return found | {(0, k): box.swap(part, "y", k) for k in range(1, ny)}

    def corner(sides):
        found = {}
        for i in range(1, nx):
            for j in range(1, ny):
                upper, lower = jnp.split(sides[i, 0], 2)[0], jnp.split(sides[0, j], 2)[1]
                found[i, j] = [box.swap(upper, "y", j), box.swap(lower, "x", i)]
        return found

    def cached(*batches):
        pieces, bases = [], []
        for first, batch in batches:
            for (i, j), held in batch.items():
                start = first
                for piece in held:
                    for k in range(2):
                        pieces.append(piece if k == 0 else box.swap(piece, "c", 1))
                        bases.append(((k * ny + j) * nx + i) * nz * share + start)
                    start += piece.shape[0]
        return kernel_call(
            functools.partial(cached_body, bases=bases),
            jax.ShapeDtypeStruct((hits, wide), BF16),
            flops=2 * hits * wide * sum(piece.shape[0] for piece in pieces),
        )(code, *pieces)

    near = lax.optimization_barrier(near)
    near_own = jnp.concatenate(near, 0)
    half = near_own.shape[0]
    near_side = side(near_own)
    far = [box.swap(near[0], "z", k) for k in range(nz // 2, nz)]
    asked, store_low, near_side = lax.optimization_barrier((asked, store_low, near_side))
    served = kernel_call(
        serve_body,
        jax.ShapeDtypeStruct((owners * cap, wide), BF16),
        flops=2 * owners * cap * store.shape[0] * wide,
    )(asked, store_low)
    served, far, hot, names = lax.optimization_barrier((served, far, hot, names))
    miss_rows = lax.all_to_all(
        served.reshape(owners, cap, wide), BOTH, split_axis=0, concat_axis=0, tiled=True
    ).reshape(owners * cap, wide)

    sel_hit, sel_miss, count, back, flags, code = kernel_call(
        functools.partial(tables_body, hits=hits),
        (
            jax.ShapeDtypeStruct((2, rows, hits), BF16),
            jax.ShapeDtypeStruct((2, rows, owners * cap), BF16),
            jax.ShapeDtypeStruct((rows, 1), F32),
            jax.ShapeDtypeStruct((rows, hid), BF16),
            jax.ShapeDtypeStruct((seeds, fan_two), F32),
            jax.ShapeDtypeStruct((hits, 1), I32),
        ),
        flops=8 * rows * misses * owners * cap,
    )(targets, names, slot, seed_mask.T, code, d_emb, w2_self, w2_nbr)

    far_own = jnp.concatenate(far, 0)
    far_side = side(far_own)
    near_corner = corner(near_side)
    first = cached((0, {(0, 0): [near_own]}), (half, {(0, 0): [far_own]}))
    second = cached((0, {at: [piece] for at, piece in near_side.items()}))
    far_side, near_corner, first, second = lax.optimization_barrier(
        (far_side, near_corner, first, second)
    )
    far_corner = corner(far_side)
    third = cached((half, {at: [piece] for at, piece in far_side.items()}), (0, near_corner))
    far_corner, third = lax.optimization_barrier((far_corner, third))
    fourth = cached((half, far_corner))
    own_part, near_part = kernel_call(
        share_body,
        (
            jax.ShapeDtypeStruct((rows, wide), BF16),
            jax.ShapeDtypeStruct((rows, wide), F32),
        ),
        flops=4 * hits * wide * rows,
    )(sel_hit, first, second, third, fourth)

    hot, own_part, near_part = lax.optimization_barrier((hot, own_part, near_part))
    far_hot = [hot] + [box.swap(hot, "y", k) for k in range(1, ny)]
    grad_scale = 1.0 / math.sqrt(seeds * owners)
    total_rows = 2 * wide + 2 * hid
    vmem, hbm = pl.BlockSpec(memory_space=pltpu.VMEM), pl.BlockSpec(memory_space=pltpu.HBM)
    streamed = (
        miss_rows, w1_self, w1_nbr, back, w2_self, w2_nbr, d_emb, sel_miss, own_part, near_part
    )
    turn = 256
    emb, send, keep = pl.pallas_call(
        functools.partial(step_body, scale=grad_scale, step=turn),
        out_shape=(
            jax.ShapeDtypeStruct((seeds, hid), BF16),
            jax.ShapeDtypeStruct((total_rows // 2, hid), BF16),
            jax.ShapeDtypeStruct((total_rows // 2, hid), F32),
        ),
        in_specs=[pl.BlockSpec(memory_space=pltpu.SMEM)] + [hbm] * 10 + [vmem] * 2,
        out_specs=(vmem,) * 3,
        scratch_shapes=[pltpu.VMEM(array.shape, array.dtype) for array in streamed]
        + [
            pltpu.VMEM((rows, wide), BF16),
            pltpu.VMEM((rows, wide), BF16),
            pltpu.VMEM((rows, hid), BF16),
            pltpu.VMEM((rows, hid), BF16),
            pltpu.SemaphoreType.DMA((7 + 3 * (rows // turn),)),
        ],
        compiler_params=pltpu.CompilerParams(vmem_limit_bytes=2 * GRANT),
        cost_estimate=pl.CostEstimate(
            flops=0, bytes_accessed=0, transcendentals=0
        ),
    )(box.at["c"].reshape(1), *streamed, count, flags)
    send, far_hot = lax.optimization_barrier((send, far_hot))

    sums = [keep, box.swap(send, "c", 1)]
    p = [term[: total_rows // 4] for term in sums]
    q = [term[total_rows // 4 :] for term in sums]
    p, q = box.scatter(p, "x"), box.scatter(q, "y")
    near_hot = [box.swap(block, "c", 1) for block in far_hot]
    p, q, near_hot = lax.optimization_barrier((p, q, near_hot))
    pairs = [join(pair, box.at["c"], BF16)[0] for pair in zip(far_hot, near_hot)]
    (new_cache,) = join(pairs, box.at["y"], F32)
    p, q = box.scatter(p, "y"), box.scatter(q, "x")
    others = range(1, nz)
    outgoing = [
        jnp.concatenate([total(box.part(p, "z", k)), total(box.part(q, "z", k))], 0).astype(BF16)
        for k in others
    ]
    summed = jnp.concatenate([total(box.part(p, "z", 0)), total(box.part(q, "z", 0))], 0)
    incoming = [box.swap(outgoing[k - 1], "z", k) for k in others]
    summed = total([summed] + incoming).astype(BF16)
    p, q = box.gather(summed, "z", parts=2)
    (p,), (q,) = lax.optimization_barrier((box.gather(p, "y"), box.gather(q, "x")))
    (p,), (q,) = lax.optimization_barrier((box.gather(p, "x"), box.gather(q, "y")))
    p, q = (p, box.swap(p, "c", 1)), (q, box.swap(q, "c", 1))
    cuts = [(0, wide), (wide, 2 * wide), (2 * wide, 2 * wide + hid), (2 * wide + hid, total_rows)]
    shapes = [jax.ShapeDtypeStruct((last - at, hid), F32) for at, last in cuts]
    grads = pl.pallas_call(
        functools.partial(finish_body, cuts=cuts),
        out_shape=shapes,
        in_specs=[pl.BlockSpec(memory_space=pltpu.SMEM)] + [vmem] * 4,
        out_specs=[hbm] * 4,
        scratch_shapes=[pltpu.VMEM(x.shape, x.dtype) for x in shapes]
        + [pltpu.SemaphoreType.DMA((4,))],
        compiler_params=pltpu.CompilerParams(vmem_limit_bytes=GRANT),
    )(box.at["c"].reshape(1), *p, *q)
    return (emb, *grads, new_cache)


def solution(mesh):
    split = P(BOTH)
    in_specs = (split, P("member")) + (split,) * 11 + (P(),) * 4 + (split,)
    out_specs = (split, P(), P(), P(), P(), P("member"))
    return jax.shard_map(
        on_device, mesh=mesh, in_specs=in_specs, out_specs=out_specs, check_vma=False
    )
```

```python
import functools
import math

import jax
import jax.numpy as jnp
from jax import lax
from jax.experimental import pallas as pl
from jax.experimental.pallas import tpu as pltpu
from jax.sharding import PartitionSpec as P

BLOCK = 128
BOTH = ("group", "member")
F32, BF16, I32 = jnp.float32, jnp.bfloat16, jnp.int32
GRANT = 29 * 1024 * 1024


def dot(a, b, ca=1, cb=0):
    return lax.dot_general(a, b, (((ca,), (cb,)), ((), ())), preferred_element_type=F32)


def iota(shape, dim):
    return lax.broadcasted_iota(I32, shape, dim)


def kernel_call(body, out_shape, scratch=(), smem=0, grant=GRANT):
    def call(*operands):
        specs = [pl.BlockSpec(memory_space=pltpu.SMEM)] * smem
        specs += [pl.BlockSpec(memory_space=pltpu.VMEM)] * (len(operands) - smem)
        return pl.pallas_call(
            body,
            out_shape=out_shape,
            in_specs=specs,
            out_specs=jax.tree.map(lambda _: pl.BlockSpec(memory_space=pltpu.VMEM), out_shape),
            scratch_shapes=list(scratch),
            compiler_params=pltpu.CompilerParams(vmem_limit_bytes=grant),
            cost_estimate=pl.CostEstimate(flops=0, bytes_accessed=0, transcendentals=0),
        )(*operands)

    return call


def request_body(owner_ref, row_ref, ids_ref, slot_ref):
    count = owner_ref.shape[1]
    owners, cap = ids_ref.shape
    flags = owner_ref[...] == iota((owners, count), 0)
    flag = flags.astype(F32).astype(BF16)
    earlier = (iota((count, count), 0) < iota((count, count), 1)).astype(F32).astype(BF16)
    rank = jnp.sum(jnp.where(flags, dot(flag, earlier), 0.0), axis=0, keepdims=True).astype(I32)
    slot_ref[...] = owner_ref[...] * cap + rank
    ranked = (rank == iota((cap, count), 0)).astype(F32).astype(BF16)
    row = row_ref[...]
    high = jnp.where(flags, (row // 128).astype(F32), 0.0).astype(BF16)
    low = jnp.where(flags, (row % 128).astype(F32), 0.0).astype(BF16)
    ids_ref[...] = (dot(high, ranked, 1, 1) * 128.0 + dot(low, ranked, 1, 1)).astype(I32)


def serve_body(ids_ref, store_ref, rows_ref):
    peers, cap = ids_ref.shape
    total, held = peers * cap, store_ref.shape[0]
    ids = ids_ref[...]
    spread = (iota((total, peers), 0) // cap == iota((total, peers), 1)).astype(F32).astype(BF16)
    high = dot(spread, (ids // 128).astype(F32).astype(BF16))
    low = dot(spread, (ids % 128).astype(F32).astype(BF16))
    here = iota((total, cap), 0) % cap == iota((total, cap), 1)
    flat = jnp.sum(jnp.where(here, high * 128.0 + low, 0.0), axis=1, keepdims=True).astype(I32)
    step = 256
    for at in range(0, total, step):
        pick = (flat[at : at + step] == iota((step, held), 1)).astype(F32).astype(BF16)
        rows_ref[at : at + step, :] = dot(pick, store_ref[...]).astype(BF16)


def tables_body(
    targets_ref, names_ref, slot_ref, mask_ref, code_ref, emb_ref, w2s_ref, w2n_ref,
    sel_hit_ref, sel_miss_ref, count_ref, back_ref, flag_ref, column_ref, *, hits,
):
    seeds, total = targets_ref.shape[1], names_ref.shape[1]
    misses = slot_ref.shape[1]
    slots = sel_miss_ref.shape[2]
    fan, fan_two = names_ref.shape[0] - 1, mask_ref.shape[0]
    one, zero = jnp.array(1, BF16), jnp.array(0, BF16)

    def columns(rows):
        rows = rows.astype(F32)
        pad = jnp.zeros((-rows.shape[0] % 8, rows.shape[1]), F32)
        return jnp.concatenate([rows, pad], 0).T if pad.shape[0] else rows.T

    column_ref[...] = columns(code_ref[...])[:, 0:1].astype(I32)
    names = names_ref[...]
    high = (names // 128).astype(F32).astype(BF16)
    low = (names % 128).astype(F32).astype(BF16)
    place = (slot_ref[...] == iota((slots, misses), 0)).astype(F32).astype(BF16)
    targets = columns(targets_ref[...]).astype(I32)
    for turn in range(fan_two + 1):
        cut = slice(turn * seeds, (turn + 1) * seeds)
        pick = (targets[:, turn : turn + 1] == iota((seeds, total), 1)).astype(F32).astype(BF16)
        named = (dot(pick, high, 1, 1) * 128.0 + dot(pick, low, 1, 1)).astype(I32) - 1
        here = named[:, 1:] >= 0
        count_ref[cut, :] = jnp.maximum(jnp.sum(here.astype(F32), axis=1, keepdims=True), 1.0)
        for first, width in ((0, hits), (hits, misses)):
            lane = (iota((seeds, width), 1) + first).astype(jnp.int16)
            own = jnp.where(named[:, 0:1].astype(jnp.int16) == lane, one, zero)
            near = jnp.zeros((seeds, width), BF16)
            for k in range(1, fan + 1):
                near = near + jnp.where(named[:, k : k + 1].astype(jnp.int16) == lane, one, zero)
            if first == 0:
                sel_hit_ref[0, cut, :] = own
                sel_hit_ref[1, cut, :] = near
            else:
                sel_miss_ref[0, cut, :] = dot(own, place, 1, 1).astype(BF16)
                sel_miss_ref[1, cut, :] = dot(near, place, 1, 1).astype(BF16)
    mask = columns(mask_ref[...])[:, :fan_two]
    flag_ref[...] = mask
    count_two = jnp.maximum(jnp.sum(mask, axis=1, keepdims=True), 1.0)
    back_ref[0:seeds, :] = dot(emb_ref[...], w2s_ref[...], 1, 1).astype(BF16)
    back_mean = (dot(emb_ref[...], w2n_ref[...], 1, 1) / count_two).astype(BF16).astype(F32)
    for k in range(fan_two):
        at = (k + 1) * seeds
        back_ref[at : at + seeds, :] = (mask[:, k : k + 1] * back_mean).astype(BF16)


def cached_body(code_ref, *refs, bases):
    pieces, held_ref = refs[:-1], refs[-1]
    step = 256

    @pl.loop(0, code_ref.shape[0] // step)
    def _(turn):
        cut = pl.ds(pl.multiple_of(turn * step, step), step)
        total = None
        for piece, base in zip(pieces, bases):
            lane = iota((step, piece.shape[0]), 1) + base
            pick = (code_ref[cut, :] == lane).astype(F32).astype(BF16)
            part = dot(pick, piece[...])
            total = part if total is None else total + part
        held_ref[cut, :] = total.astype(BF16)


def share_body(sel_ref, *refs):
    parts, (own_ref, near_ref) = refs[:-2], refs[-2:]
    held = parts[0][...]
    for part in parts[1:]:
        held = held + part[...]
    step = 256
    for at in range(0, own_ref.shape[0], step):
        own_ref[at : at + step, :] = dot(sel_ref[0, at : at + step, :], held).astype(BF16)
        near_ref[at : at + step, :] = dot(sel_ref[1, at : at + step, :], held)


def join_body(me_ref, *refs, count, parts):
    pieces, outs = refs[:count], refs[count:]
    for k in range(count):
        depth = pieces[k].shape[0] // parts
        place = pl.multiple_of((me_ref[0] ^ k) * depth, 16)
        for j in range(parts):
            value = pieces[k][j * depth : (j + 1) * depth, :]
            outs[j][pl.ds(place, depth), :] = value.astype(outs[j].dtype)


def join(pieces, me, dtype, parts=1):
    count = len(pieces)
    depth, width = pieces[0].shape[0] // parts, pieces[0].shape[1]
    if depth % 16 == 0:
        return kernel_call(
            functools.partial(join_body, count=count, parts=parts),
            [jax.ShapeDtypeStruct((count * depth, width), dtype)] * parts,
            smem=1,
        )(me.reshape(1), *pieces)
    outs = [jnp.zeros((count * depth, width), dtype)] * parts
    for k in range(count):
        for j in range(parts):
            value = pieces[k][j * depth : (j + 1) * depth].astype(dtype)
            outs[j] = lax.dynamic_update_slice_in_dim(outs[j], value, (me ^ k) * depth, 0)
    return outs


def step_body(core_ref, *refs, scale, step):
    sources, (count_ref, mask_ref, out_ref, *refs) = refs[:10], refs[10:]
    send_refs, keep_refs, refs = refs[:2], refs[2:4], refs[4:]
    held, (self_ref, mean_ref, hid_ref, bp_ref, sems) = refs[:10], refs[10:]
    miss_ref, w1s_ref, w1n_ref, back_ref, w2s_ref, w2n_ref, emb_ref, *turned = held
    sel_ref, own_ref, near_ref = turned
    rows, wide = own_ref.shape
    seeds = mask_ref.shape[0]
    hid = w1s_ref.shape[1]
    turns = rows // step

    def copy(i, turn=None):
        source, target, number = sources[i], held[i], i
        if turn is not None:
            cut = slice(turn * step, (turn + 1) * step)
            source, target = (
                (ref.at[:, cut, :] if len(ref.shape) == 3 else ref.at[cut, :])
                for ref in (source, target)
            )
            number = 7 + (i - 7) * turns + turn
        return pltpu.make_async_copy(source, target, sems.at[number])

    order = [(0,), (7, 0), (8, 0), (9, 0), (1,), (2,), (3,)]
    order += [(i, turn) for turn in range(1, turns) for i in (7, 8, 9)] + [(4,), (5,), (6,)]
    for item in order:
        copy(*item).start()
    copy(0).wait()
    for turn in range(turns):
        cut = slice(turn * step, (turn + 1) * step)
        copy(7, turn).wait()
        own = dot(sel_ref[0, cut, :], miss_ref[...])
        near = dot(sel_ref[1, cut, :], miss_ref[...])
        copy(8, turn).wait()
        copy(9, turn).wait()
        own = (own_ref[cut, :].astype(F32) + own).astype(BF16)
        mean = ((near_ref[cut, :] + near) / count_ref[cut, :]).astype(BF16)
        self_ref[cut, :] = own
        mean_ref[cut, :] = mean
        if turn == 0:
            copy(1).wait()
            copy(2).wait()
        pre = dot(own, w1s_ref[...]) + dot(mean, w1n_ref[...])
        gate = jax.nn.sigmoid(pre)
        hid_ref[cut, :] = (pre * gate).astype(BF16)
        slope = gate * (1.0 + pre * (1.0 - gate))
        if turn == 0:
            copy(3).wait()
        bp_ref[cut, :] = (back_ref[cut, :].astype(F32) * slope).astype(BF16)

    core = core_ref[0]
    quarter = keep_refs[0].shape[0]

    def put(at, value):
        value = value * scale
        first = 0
        while first < value.shape[0]:
            number, place = (at + first) // quarter, (at + first) % quarter
            depth = min(value.shape[0] - first, quarter - place)
            part, rows_at = value[first : first + depth], slice(place, place + depth)

            @pl.when(core == number // 2)
            def _(part=part, rows_at=rows_at, ref=keep_refs[number % 2]):
                ref[rows_at, :] = part.astype(BF16)

            @pl.when(core != number // 2)
            def _(part=part, rows_at=rows_at, ref=send_refs[number % 2]):
                ref[rows_at, :] = part.astype(BF16)

            first += depth

    mask = mask_ref[...]
    count_two = jnp.maximum(jnp.sum(mask, axis=1, keepdims=True), 1.0)
    total = jnp.zeros((seeds, hid), F32)
    for k in range(mask.shape[1]):
        at = (k + 1) * seeds
        total = total + mask[:, k : k + 1] * hid_ref[at : at + seeds, :].astype(F32)
    mean_two = (total / count_two).astype(BF16)
    self_two = hid_ref[0:seeds, :]
    for i in (4, 5, 6):
        copy(i).wait()
    out_ref[...] = (dot(self_two, w2s_ref[...]) + dot(mean_two, w2n_ref[...])).astype(BF16)
    put(2 * wide, dot(self_two, emb_ref[...], 0, 0))
    put(2 * wide + hid, dot(mean_two, emb_ref[...], 0, 0))
    for base, ref in ((0, self_ref), (wide, mean_ref)):
        for at in range(0, wide, step):
            put(base + at, dot(ref[:, at : at + step], bp_ref[...], 0, 0))


def fold_body(me_ref, *refs, terms, counts, together):
    ins, outs = refs[: sum(terms)], refs[sum(terms) :]
    for i, count in enumerate(counts):
        held, ins = ins[: terms[i]], ins[terms[i] :]
        depth = held[0].shape[0] // count
        for k in range(count):
            place = pl.ds(pl.multiple_of((me_ref[i] ^ k) * depth, 16), depth)
            value = held[0][place, :].astype(F32)
            for term in held[1:]:
                value = value + term[place, :].astype(F32)
            if together:
                outs[k][i * depth : (i + 1) * depth, :] = value.astype(outs[k].dtype)
            else:
                outs[k][...] = value.astype(outs[k].dtype)
        if not together:
            outs = outs[count:]


def fold(chains, counts, me, together):
    width = chains[0][0].shape[1]
    depths = [chain[0].shape[0] // count for chain, count in zip(chains, counts)]
    if all(depth % 16 == 0 for depth in depths):
        groups = [(sum(depths), counts[0])] if together else list(zip(depths, counts))
        shapes = [
            jax.ShapeDtypeStruct((depth, width), BF16 if k else F32)
            for depth, count in groups
            for k in range(count)
        ]
        out = iter(kernel_call(
            functools.partial(
                fold_body, terms=[len(c) for c in chains], counts=counts, together=together
            ),
            shapes,
            smem=1,
        )(jnp.stack(me), *[term for chain in chains for term in chain]))
        return [[next(out) for _ in range(count)] for _, count in groups]
    found = []
    for chain, count, depth, at in zip(chains, counts, depths, me):
        parts = [
            total([lax.dynamic_slice_in_dim(t, (at ^ k) * depth, depth, 0) for t in chain])
            for k in range(count)
        ]
        found.append([part.astype(BF16) if k else part for k, part in enumerate(parts)])
    return [[jnp.concatenate(pair, 0) for pair in zip(*found)]] if together else found


def finish_body(core_ref, *refs, cuts):
    (p, p_far, q, q_far), outs, held, sems = refs[:4], refs[4:8], refs[8:12], refs[12]
    quarter = p.shape[0]
    for near_core in range(2):

        @pl.when(core_ref[0] == near_core)
        def _():
            order = [(p, p_far), (q, q_far)]
            order = [pair[core != near_core] for core in range(2) for pair in order]
            for i, (first, last) in enumerate(cuts):
                at = first
                while at < last:
                    number, place = at // quarter, at % quarter
                    upto = min(last, (number + 1) * quarter)
                    held[i][at - first : upto - first, :] = order[number][
                        place : place + upto - at, :
                    ].astype(F32)
                    at = upto
                pltpu.make_async_copy(held[i], outs[i], sems.at[i]).start()

    for i in range(len(cuts)):
        pltpu.make_async_copy(held[i], outs[i], sems.at[i]).wait()


class Slice:
    def __init__(self):
        self.groups, self.members = lax.axis_size("group"), lax.axis_size("member")
        self.size = {"c": 2, "y": self.groups // 2, "z": 4, "x": self.members // 4}
        group, member = lax.axis_index("group"), lax.axis_index("member")
        self.at = {
            "c": group % 2,
            "y": group // 2,
            "z": member // self.size["x"],
            "x": member % self.size["x"],
        }

    def swap(self, array, axis, k):
        stride = {"c": 1, "y": 2, "z": self.size["x"], "x": 1}[axis]
        name, count = ("group", self.groups) if axis in "cy" else ("member", self.members)
        return lax.ppermute(array, name, [(i, i ^ (k * stride)) for i in range(count)])

    def scatter(self, chains, axes, together=False):
        out = fold(chains, [self.size[a] for a in axes], [self.at[a] for a in axes], together)
        if together:
            axes = axes[:1]
        return [
            [mine] + [self.swap(part, axis, k + 1) for k, part in enumerate(parts)]
            for (mine, *parts), axis in zip(out, axes)
        ]

    def gather(self, part, axis, dtype=BF16, parts=1):
        pieces = [part] + [self.swap(part, axis, k) for k in range(1, self.size[axis])]
        return join(pieces, self.at[axis], dtype, parts)


def total(terms):
    out = terms[0].astype(F32)
    for term in terms[1:]:
        out = out + term.astype(F32)
    return out


def on_device(
    store,
    cache,
    hot_local,
    hit_member,
    hit_row,
    miss_owner,
    miss_row,
    tgt_self,
    tgt_nbr,
    tgt_mask,
    seed_self,
    seed_nbr,
    seed_mask,
    w1_self,
    w1_nbr,
    w2_self,
    w2_nbr,
    d_emb,
):
    box = Slice()
    nx, ny, nz = box.size["x"], box.size["y"], box.size["z"]
    wide, hid = w1_self.shape
    owners = box.groups * box.members
    hits, misses = hit_row.shape[0], miss_row.shape[0]
    cap = 2 * misses // owners
    seeds, fan_two = seed_nbr.shape
    rows = seeds * (fan_two + 1)

    share = cache.shape[0] // box.groups
    group = lax.axis_index("group")
    mine = lax.dynamic_slice_in_dim(cache, group * share, share, 0).astype(BF16)

    ids, slot = kernel_call(
        request_body,
        (
            jax.ShapeDtypeStruct((owners, cap), I32),
            jax.ShapeDtypeStruct((1, misses), I32),
        ),
    )(miss_owner.reshape(1, -1), miss_row.reshape(1, -1))
    store_low = store.astype(BF16)
    asked = lax.all_to_all(
        ids.reshape(owners, 1, cap), BOTH, split_axis=0, concat_axis=0, tiled=True
    ).reshape(owners, cap)
    near = [mine] + [box.swap(mine, "z", k) for k in range(1, nz // 2)]

    targets = jnp.concatenate([seed_self[None, :], seed_nbr.T], 0)
    names = jnp.concatenate([tgt_self[None, :] + 1, jnp.where(tgt_mask > 0, tgt_nbr + 1, 0).T], 0)
    member, line = hit_member.reshape(1, -1), hit_row.reshape(1, -1)
    holder = line // share
    code = ((holder % 2) ^ box.at["c"]) * ny + ((holder // 2) ^ box.at["y"])
    code = code * nx + ((member % nx) ^ box.at["x"])
    code = code * nz + ((member // nx) ^ box.at["z"])
    code = code * share + line % share
    hot = lax.dynamic_slice_in_dim(store, hot_local[0, 0] * BLOCK, BLOCK, 0).astype(BF16)

    def side(part):
        found = {(k, 0): box.swap(part, "x", k) for k in range(1, nx)}
        return found | {(0, k): box.swap(part, "y", k) for k in range(1, ny)}

    def corner(sides, way=0):
        found = {}
        for i in range(1, nx):
            for j in range(1, ny):
                if way:
                    found[i, j] = [box.swap(sides[i, 0], "y", j) if way == 1 else box.swap(sides[0, j], "x", i)]
                    continue
                upper, lower = jnp.split(sides[i, 0], 2)[0], jnp.split(sides[0, j], 2)[1]
                found[i, j] = [box.swap(upper, "y", j), box.swap(lower, "x", i)]
        return found

    def cached(*batches):
        pieces, bases = [], []
        for first, batch in batches:
            for (i, j), held in batch.items():
                start = first
                for piece in held:
                    for k in range(2):
                        pieces.append(piece if k == 0 else box.swap(piece, "c", 1))
                        bases.append(((k * ny + j) * nx + i) * nz * share + start)
                    start += piece.shape[0]
        return kernel_call(
            functools.partial(cached_body, bases=bases),
            jax.ShapeDtypeStruct((hits, wide), BF16),
        )(code, *pieces)

    far = [box.swap(mine, "z", k) for k in range(nz // 2, nz - 1)]
    near = lax.optimization_barrier(near)
    near_own = jnp.concatenate(near, 0)
    half = near_own.shape[0]
    near_side = side(near_own)
    far.append(box.swap(near[0], "z", nz - 1))
    asked, store_low, near_side = lax.optimization_barrier((asked, store_low, near_side))
    served = kernel_call(
        serve_body,
        jax.ShapeDtypeStruct((owners * cap, wide), BF16),
    )(asked, store_low)
    near_corner = corner(near_side, 1)
    served, far, hot, names = lax.optimization_barrier((served, far, hot, names))
    miss_rows = lax.all_to_all(
        served.reshape(owners, cap, wide), BOTH, split_axis=0, concat_axis=0, tiled=True
    ).reshape(owners * cap, wide)

    sel_hit, sel_miss, count, back, flags, code = kernel_call(
        functools.partial(tables_body, hits=hits),
        (
            jax.ShapeDtypeStruct((2, rows, hits), BF16),
            jax.ShapeDtypeStruct((2, rows, owners * cap), BF16),
            jax.ShapeDtypeStruct((rows, 1), F32),
            jax.ShapeDtypeStruct((rows, hid), BF16),
            jax.ShapeDtypeStruct((seeds, fan_two), F32),
            jax.ShapeDtypeStruct((hits, 1), I32),
        ),
    )(targets, names, slot, seed_mask.T, code, d_emb, w2_self, w2_nbr)

    far_own = jnp.concatenate(far, 0)
    far_side = side(far_own)
    first = cached((0, {(0, 0): [near_own]}), (half, {(0, 0): [far_own]}))
    second = cached((0, {at: [piece] for at, piece in near_side.items()}))
    far_side, first, second = lax.optimization_barrier((far_side, first, second))
    far_corner = corner(far_side, 2)
    third = cached((half, {at: [piece] for at, piece in far_side.items()}))
    near_corner, far_corner, third = lax.optimization_barrier((near_corner, far_corner, third))
    fourth = cached((0, near_corner), (half, far_corner))
    own_part, near_part = kernel_call(
        share_body,
        (
            jax.ShapeDtypeStruct((rows, wide), BF16),
            jax.ShapeDtypeStruct((rows, wide), F32),
        ),
    )(sel_hit, first, second, third, fourth)

    hot, own_part, near_part = lax.optimization_barrier((hot, own_part, near_part))
    far_hot = [hot] + [box.swap(hot, "y", k) for k in range(1, ny)]
    grad_scale = 1.0 / math.sqrt(seeds * owners)
    total_rows = 2 * wide + 2 * hid
    vmem, hbm = pl.BlockSpec(memory_space=pltpu.VMEM), pl.BlockSpec(memory_space=pltpu.HBM)
    streamed = (
        miss_rows, w1_self, w1_nbr, back, w2_self, w2_nbr, d_emb, sel_miss, own_part, near_part
    )
    turn = 256
    emb, *sums = pl.pallas_call(
        functools.partial(step_body, scale=grad_scale, step=turn),
        out_shape=(
            jax.ShapeDtypeStruct((seeds, hid), BF16),
            *[jax.ShapeDtypeStruct((total_rows // 4, hid), kind) for kind in (BF16,) * 4],
        ),
        in_specs=[pl.BlockSpec(memory_space=pltpu.SMEM)] + [hbm] * 10 + [vmem] * 2,
        out_specs=(vmem,) * 5,
        scratch_shapes=[pltpu.VMEM(array.shape, array.dtype) for array in streamed]
        + [
            pltpu.VMEM((rows, wide), BF16),
            pltpu.VMEM((rows, wide), BF16),
            pltpu.VMEM((rows, hid), BF16),
            pltpu.VMEM((rows, hid), BF16),
            pltpu.SemaphoreType.DMA((7 + 3 * (rows // turn),)),
        ],
        compiler_params=pltpu.CompilerParams(vmem_limit_bytes=2 * GRANT),
        cost_estimate=pl.CostEstimate(
            flops=0, bytes_accessed=0, transcendentals=0
        ),
    )(box.at["c"].reshape(1), *streamed, count, flags)
    sums, far_hot = lax.optimization_barrier((sums, far_hot))

    p, q = ([sums[2 + i], box.swap(sums[i], "c", 1)] for i in range(2))
    p, q = box.scatter((p, q), ("x", "y"))
    near_hot = [box.swap(block, "c", 1) for block in far_hot]
    p, q, near_hot = lax.optimization_barrier((p, q, near_hot))
    pairs = [join(pair, box.at["c"], BF16)[0] for pair in zip(far_hot, near_hot)]
    (new_cache,) = join(pairs, box.at["y"], F32)
    p, q = box.scatter((p, q), ("y", "x"))
    (summed,) = box.scatter((p, q), ("z", "z"), together=True)
    summed = total(summed).astype(BF16)
    p, q = box.gather(summed, "z", parts=2)
    (p,), (q,) = lax.optimization_barrier((box.gather(p, "y"), box.gather(q, "x")))
    (p,), (q,) = lax.optimization_barrier((box.gather(p, "x"), box.gather(q, "y")))
    p, q = (p, box.swap(p, "c", 1)), (q, box.swap(q, "c", 1))
    cuts = [(0, wide), (wide, 2 * wide), (2 * wide, 2 * wide + hid), (2 * wide + hid, total_rows)]
    shapes = [jax.ShapeDtypeStruct((last - at, hid), F32) for at, last in cuts]
    grads = pl.pallas_call(
        functools.partial(finish_body, cuts=cuts),
        out_shape=shapes,
        in_specs=[pl.BlockSpec(memory_space=pltpu.SMEM)] + [vmem] * 4,
        out_specs=[hbm] * 4,
        scratch_shapes=[pltpu.VMEM(x.shape, x.dtype) for x in shapes]
        + [pltpu.SemaphoreType.DMA((4,))],
        compiler_params=pltpu.CompilerParams(vmem_limit_bytes=GRANT),
    )(box.at["c"].reshape(1), *p, *q)
    return (emb, *grads, new_cache)


def solution(mesh):
    split = P(BOTH)
    in_specs = (split, P("member")) + (split,) * 11 + (P(),) * 4 + (split,)
    out_specs = (split, P(), P(), P(), P(), P("member"))
    return jax.shard_map(
        on_device, mesh=mesh, in_specs=in_specs, out_specs=out_specs, check_vma=False
    )
```

```python
import functools
import math

import jax
import jax.numpy as jnp
from jax import lax
from jax.experimental import pallas as pl
from jax.experimental.pallas import tpu as pltpu
from jax.sharding import PartitionSpec as P

BLOCK = 128
BOTH = ("group", "member")
F32, BF16, I32 = jnp.float32, jnp.bfloat16, jnp.int32
GRANT = 29 * 1024 * 1024


def dot(a, b, ca=1, cb=0):
    return lax.dot_general(a, b, (((ca,), (cb,)), ((), ())), preferred_element_type=F32)


def iota(shape, dim):
    return lax.broadcasted_iota(I32, shape, dim)


def kernel_call(body, out_shape, scratch=(), smem=0, grant=GRANT):
    def call(*operands):
        specs = [pl.BlockSpec(memory_space=pltpu.SMEM)] * smem
        specs += [pl.BlockSpec(memory_space=pltpu.VMEM)] * (len(operands) - smem)
        return pl.pallas_call(
            body,
            out_shape=out_shape,
            in_specs=specs,
            out_specs=jax.tree.map(lambda _: pl.BlockSpec(memory_space=pltpu.VMEM), out_shape),
            scratch_shapes=list(scratch),
            compiler_params=pltpu.CompilerParams(vmem_limit_bytes=grant),
            cost_estimate=pl.CostEstimate(flops=0, bytes_accessed=0, transcendentals=0),
        )(*operands)

    return call


def request_body(owner_ref, row_ref, ids_ref, slot_ref):
    count = owner_ref.shape[1]
    owners, cap = ids_ref.shape
    flags = owner_ref[...] == iota((owners, count), 0)
    flag = flags.astype(F32).astype(BF16)
    earlier = (iota((count, count), 0) < iota((count, count), 1)).astype(F32).astype(BF16)
    rank = jnp.sum(jnp.where(flags, dot(flag, earlier), 0.0), axis=0, keepdims=True).astype(I32)
    slot_ref[...] = owner_ref[...] * cap + rank
    ranked = (rank == iota((cap, count), 0)).astype(F32).astype(BF16)
    row = row_ref[...]
    high = jnp.where(flags, (row // 128).astype(F32), 0.0).astype(BF16)
    low = jnp.where(flags, (row % 128).astype(F32), 0.0).astype(BF16)
    ids_ref[...] = (dot(high, ranked, 1, 1) * 128.0 + dot(low, ranked, 1, 1)).astype(I32)


def serve_body(ids_ref, store_ref, rows_ref):
    peers, cap = ids_ref.shape
    total, held = peers * cap, store_ref.shape[0]
    ids = ids_ref[...]
    spread = (iota((total, peers), 0) // cap == iota((total, peers), 1)).astype(F32).astype(BF16)
    high = dot(spread, (ids // 128).astype(F32).astype(BF16))
    low = dot(spread, (ids % 128).astype(F32).astype(BF16))
    here = iota((total, cap), 0) % cap == iota((total, cap), 1)
    flat = jnp.sum(jnp.where(here, high * 128.0 + low, 0.0), axis=1, keepdims=True).astype(I32)
    step = 256
    for at in range(0, total, step):
        pick = (flat[at : at + step] == iota((step, held), 1)).astype(F32).astype(BF16)
        rows_ref[at : at + step, :] = dot(pick, store_ref[...]).astype(BF16)


def tables_body(
    targets_ref, names_ref, slot_ref, mask_ref, code_ref, emb_ref, w2s_ref, w2n_ref,
    sel_hit_ref, sel_miss_ref, count_ref, back_ref, flag_ref, column_ref, *, hits,
):
    seeds, total = targets_ref.shape[1], names_ref.shape[1]
    misses = slot_ref.shape[1]
    slots = sel_miss_ref.shape[2]
    fan, fan_two = names_ref.shape[0] - 1, mask_ref.shape[0]
    one, zero = jnp.array(1, BF16), jnp.array(0, BF16)

    def columns(rows):
        rows = rows.astype(F32)
        pad = jnp.zeros((-rows.shape[0] % 8, rows.shape[1]), F32)
        return jnp.concatenate([rows, pad], 0).T if pad.shape[0] else rows.T

    column_ref[...] = columns(code_ref[...])[:, 0:1].astype(I32)
    names = names_ref[...]
    high = (names // 128).astype(F32).astype(BF16)
    low = (names % 128).astype(F32).astype(BF16)
    place = (slot_ref[...] == iota((slots, misses), 0)).astype(F32).astype(BF16)
    targets = columns(targets_ref[...]).astype(I32)
    for turn in range(fan_two + 1):
        cut = slice(turn * seeds, (turn + 1) * seeds)
        pick = (targets[:, turn : turn + 1] == iota((seeds, total), 1)).astype(F32).astype(BF16)
        named = (dot(pick, high, 1, 1) * 128.0 + dot(pick, low, 1, 1)).astype(I32) - 1
        here = named[:, 1:] >= 0
        count_ref[cut, :] = jnp.maximum(jnp.sum(here.astype(F32), axis=1, keepdims=True), 1.0)
        for first, width in ((0, hits), (hits, misses)):
            lane = (iota((seeds, width), 1) + first).astype(jnp.int16)
            own = jnp.where(named[:, 0:1].astype(jnp.int16) == lane, one, zero)
            near = jnp.zeros((seeds, width), BF16)
            for k in range(1, fan + 1):
                near = near + jnp.where(named[:, k : k + 1].astype(jnp.int16) == lane, one, zero)
            if first == 0:
                sel_hit_ref[0, cut, :] = own
                sel_hit_ref[1, cut, :] = near
            else:
                sel_miss_ref[0, cut, :] = dot(own, place, 1, 1).astype(BF16)
                sel_miss_ref[1, cut, :] = dot(near, place, 1, 1).astype(BF16)
    mask = columns(mask_ref[...])[:, :fan_two]
    flag_ref[...] = mask
    count_two = jnp.maximum(jnp.sum(mask, axis=1, keepdims=True), 1.0)
    back_ref[0:seeds, :] = dot(emb_ref[...], w2s_ref[...], 1, 1).astype(BF16)
    back_mean = (dot(emb_ref[...], w2n_ref[...], 1, 1) / count_two).astype(BF16).astype(F32)
    for k in range(fan_two):
        at = (k + 1) * seeds
        back_ref[at : at + seeds, :] = (mask[:, k : k + 1] * back_mean).astype(BF16)


def cached_body(code_ref, *refs, bases):
    pieces, held_ref = refs[:-1], refs[-1]
    step = 256
    groups, depth = [], step
    for i, piece in enumerate(pieces):
        if depth + piece.shape[0] > step:
            groups, depth = groups + [[]], 0
        groups[-1].append(i)
        depth += piece.shape[0]

    @pl.loop(0, code_ref.shape[0] // step)
    def _(turn):
        cut = pl.ds(pl.multiple_of(turn * step, step), step)
        total = None
        for group in groups:
            lanes = [iota((step, pieces[i].shape[0]), 1) + bases[i] for i in group]
            lane = lanes[0] if len(group) == 1 else jnp.concatenate(lanes, 1)
            rows = [pieces[i][...] for i in group]
            pick = (code_ref[cut, :] == lane).astype(F32).astype(BF16)
            part = dot(pick, rows[0] if len(group) == 1 else jnp.concatenate(rows, 0))
            total = part if total is None else total + part
        held_ref[cut, :] = total.astype(BF16)


def share_body(sel_ref, *refs):
    parts, (own_ref, near_ref) = refs[:-2], refs[-2:]
    held = parts[0][...]
    for part in parts[1:]:
        held = held + part[...]
    step = 256
    for at in range(0, own_ref.shape[0], step):
        own_ref[at : at + step, :] = dot(sel_ref[0, at : at + step, :], held).astype(BF16)
        near_ref[at : at + step, :] = dot(sel_ref[1, at : at + step, :], held)


def join_body(me_ref, *refs, count, parts):
    pieces, outs = refs[:count], refs[count:]
    for k in range(count):
        depth = pieces[k].shape[0] // parts
        place = pl.multiple_of((me_ref[0] ^ k) * depth, 16)
        for j in range(parts):
            value = pieces[k][j * depth : (j + 1) * depth, :]
            outs[j][pl.ds(place, depth), :] = value.astype(outs[j].dtype)


def join(pieces, me, dtype, parts=1):
    count = len(pieces)
    depth, width = pieces[0].shape[0] // parts, pieces[0].shape[1]
    if depth % 16 == 0:
        return kernel_call(
            functools.partial(join_body, count=count, parts=parts),
            [jax.ShapeDtypeStruct((count * depth, width), dtype)] * parts,
            smem=1,
        )(me.reshape(1), *pieces)
    outs = [jnp.zeros((count * depth, width), dtype)] * parts
    for k in range(count):
        for j in range(parts):
            value = pieces[k][j * depth : (j + 1) * depth].astype(dtype)
            outs[j] = lax.dynamic_update_slice_in_dim(outs[j], value, (me ^ k) * depth, 0)
    return outs


def step_body(core_ref, *refs, scale, step):
    sources, (count_ref, mask_ref, out_ref, *refs) = refs[:10], refs[10:]
    send_refs, keep_refs, refs = refs[:2], refs[2:4], refs[4:]
    held, (self_ref, mean_ref, hid_ref, bp_ref, sems) = refs[:10], refs[10:]
    miss_ref, w1s_ref, w1n_ref, back_ref, w2s_ref, w2n_ref, emb_ref, *turned = held
    sel_ref, own_ref, near_ref = turned
    rows, wide = own_ref.shape
    seeds = mask_ref.shape[0]
    hid = w1s_ref.shape[1]
    turns = rows // step

    def copy(i, turn=None):
        source, target, number = sources[i], held[i], i
        if turn is not None:
            cut = slice(turn * step, (turn + 1) * step)
            source, target = (
                (ref.at[:, cut, :] if len(ref.shape) == 3 else ref.at[cut, :])
                for ref in (source, target)
            )
            number = 7 + (i - 7) * turns + turn
        return pltpu.make_async_copy(source, target, sems.at[number])

    order = [(0,), (7, 0), (8, 0), (9, 0), (1,), (2,), (3,)]
    order += [(i, turn) for turn in range(1, turns) for i in (7, 8, 9)] + [(4,), (5,), (6,)]
    for item in order:
        copy(*item).start()
    copy(0).wait()
    for turn in range(turns):
        cut = slice(turn * step, (turn + 1) * step)
        copy(7, turn).wait()
        own = dot(sel_ref[0, cut, :], miss_ref[...])
        near = dot(sel_ref[1, cut, :], miss_ref[...])
        copy(8, turn).wait()
        copy(9, turn).wait()
        own = (own_ref[cut, :].astype(F32) + own).astype(BF16)
        mean = ((near_ref[cut, :] + near) / count_ref[cut, :]).astype(BF16)
        self_ref[cut, :] = own
        mean_ref[cut, :] = mean
        if turn == 0:
            copy(1).wait()
            copy(2).wait()
        pre = dot(own, w1s_ref[...]) + dot(mean, w1n_ref[...])
        gate = jax.nn.sigmoid(pre)
        hid_ref[cut, :] = (pre * gate).astype(BF16)
        slope = gate * (1.0 + pre * (1.0 - gate))
        if turn == 0:
            copy(3).wait()
        bp_ref[cut, :] = (back_ref[cut, :].astype(F32) * slope).astype(BF16)

    core = core_ref[0]
    quarter = keep_refs[0].shape[0]

    def put(at, value):
        value = value * scale
        first = 0
        while first < value.shape[0]:
            number, place = (at + first) // quarter, (at + first) % quarter
            depth = min(value.shape[0] - first, quarter - place)
            part, rows_at = value[first : first + depth], slice(place, place + depth)

            @pl.when(core == number // 2)
            def _(part=part, rows_at=rows_at, ref=keep_refs[number % 2]):
                ref[rows_at, :] = part.astype(BF16)

            @pl.when(core != number // 2)
            def _(part=part, rows_at=rows_at, ref=send_refs[number % 2]):
                ref[rows_at, :] = part.astype(BF16)

            first += depth

    mask = mask_ref[...]
    count_two = jnp.maximum(jnp.sum(mask, axis=1, keepdims=True), 1.0)
    total = jnp.zeros((seeds, hid), F32)
    for k in range(mask.shape[1]):
        at = (k + 1) * seeds
        total = total + mask[:, k : k + 1] * hid_ref[at : at + seeds, :].astype(F32)
    mean_two = (total / count_two).astype(BF16)
    self_two = hid_ref[0:seeds, :]
    for i in (4, 5, 6):
        copy(i).wait()
    out_ref[...] = (dot(self_two, w2s_ref[...]) + dot(mean_two, w2n_ref[...])).astype(BF16)
    put(2 * wide, dot(self_two, emb_ref[...], 0, 0))
    put(2 * wide + hid, dot(mean_two, emb_ref[...], 0, 0))
    for base, ref in ((0, self_ref), (wide, mean_ref)):
        for at in range(0, wide, step):
            put(base + at, dot(ref[:, at : at + step], bp_ref[...], 0, 0))


def fold_body(me_ref, *refs, terms, counts, together):
    ins, outs = refs[: sum(terms)], refs[sum(terms) :]
    for i, count in enumerate(counts):
        held, ins = ins[: terms[i]], ins[terms[i] :]
        depth = held[0].shape[0] // count
        for k in range(count):
            place = pl.ds(pl.multiple_of((me_ref[i] ^ k) * depth, 16), depth)
            value = held[0][place, :].astype(F32)
            for term in held[1:]:
                value = value + term[place, :].astype(F32)
            if together:
                outs[k][i * depth : (i + 1) * depth, :] = value.astype(outs[k].dtype)
            else:
                outs[k][...] = value.astype(outs[k].dtype)
        if not together:
            outs = outs[count:]


def fold(chains, counts, me, together):
    width = chains[0][0].shape[1]
    depths = [chain[0].shape[0] // count for chain, count in zip(chains, counts)]
    if all(depth % 16 == 0 for depth in depths):
        groups = [(sum(depths), counts[0])] if together else list(zip(depths, counts))
        shapes = [
            jax.ShapeDtypeStruct((depth, width), BF16 if k else F32)
            for depth, count in groups
            for k in range(count)
        ]
        out = iter(kernel_call(
            functools.partial(
                fold_body, terms=[len(c) for c in chains], counts=counts, together=together
            ),
            shapes,
            smem=1,
        )(jnp.stack(me), *[term for chain in chains for term in chain]))
        return [[next(out) for _ in range(count)] for _, count in groups]
    found = []
    for chain, count, depth, at in zip(chains, counts, depths, me):
        parts = [
            total([lax.dynamic_slice_in_dim(t, (at ^ k) * depth, depth, 0) for t in chain])
            for k in range(count)
        ]
        found.append([part.astype(BF16) if k else part for k, part in enumerate(parts)])
    return [[jnp.concatenate(pair, 0) for pair in zip(*found)]] if together else found


def finish_body(core_ref, *refs, cuts):
    (p, p_far, q, q_far), outs, held, sems = refs[:4], refs[4:8], refs[8:12], refs[12]
    quarter = p.shape[0]
    for near_core in range(2):

        @pl.when(core_ref[0] == near_core)
        def _():
            order = [(p, p_far), (q, q_far)]
            order = [pair[core != near_core] for core in range(2) for pair in order]
            for i, (first, last) in enumerate(cuts):
                at = first
                while at < last:
                    number, place = at // quarter, at % quarter
                    upto = min(last, (number + 1) * quarter)
                    held[i][at - first : upto - first, :] = order[number][
                        place : place + upto - at, :
                    ].astype(F32)
                    at = upto
                pltpu.make_async_copy(held[i], outs[i], sems.at[i]).start()

    for i in range(len(cuts)):
        pltpu.make_async_copy(held[i], outs[i], sems.at[i]).wait()


class Slice:
    def __init__(self):
        self.groups, self.members = lax.axis_size("group"), lax.axis_size("member")
        self.size = {"c": 2, "y": self.groups // 2, "z": 4, "x": self.members // 4}
        group, member = lax.axis_index("group"), lax.axis_index("member")
        self.at = {
            "c": group % 2,
            "y": group // 2,
            "z": member // self.size["x"],
            "x": member % self.size["x"],
        }

    def swap(self, array, axis, k):
        stride = {"c": 1, "y": 2, "z": self.size["x"], "x": 1}[axis]
        name, count = ("group", self.groups) if axis in "cy" else ("member", self.members)
        return lax.ppermute(array, name, [(i, i ^ (k * stride)) for i in range(count)])

    def scatter(self, chains, axes, together=False):
        out = fold(chains, [self.size[a] for a in axes], [self.at[a] for a in axes], together)
        if together:
            axes = axes[:1]
        return [
            [mine] + [self.swap(part, axis, k + 1) for k, part in enumerate(parts)]
            for (mine, *parts), axis in zip(out, axes)
        ]

    def gather(self, part, axis, dtype=BF16, parts=1):
        pieces = [part] + [self.swap(part, axis, k) for k in range(1, self.size[axis])]
        return join(pieces, self.at[axis], dtype, parts)


def total(terms):
    out = terms[0].astype(F32)
    for term in terms[1:]:
        out = out + term.astype(F32)
    return out


def on_device(
    store,
    cache,
    hot_local,
    hit_member,
    hit_row,
    miss_owner,
    miss_row,
    tgt_self,
    tgt_nbr,
    tgt_mask,
    seed_self,
    seed_nbr,
    seed_mask,
    w1_self,
    w1_nbr,
    w2_self,
    w2_nbr,
    d_emb,
):
    box = Slice()
    nx, ny, nz = box.size["x"], box.size["y"], box.size["z"]
    wide, hid = w1_self.shape
    owners = box.groups * box.members
    hits, misses = hit_row.shape[0], miss_row.shape[0]
    cap = 2 * misses // owners
    seeds, fan_two = seed_nbr.shape
    rows = seeds * (fan_two + 1)

    share = cache.shape[0] // box.groups
    group = lax.axis_index("group")

    def cast_share(number):
        return lax.dynamic_slice_in_dim(cache, number * share, share, 0).astype(BF16)

    mine = cast_share(group)

    ids, slot = kernel_call(
        request_body,
        (
            jax.ShapeDtypeStruct((owners, cap), I32),
            jax.ShapeDtypeStruct((1, misses), I32),
        ),
    )(miss_owner.reshape(1, -1), miss_row.reshape(1, -1))
    store_low = store.astype(BF16)
    asked = lax.all_to_all(
        ids.reshape(owners, 1, cap), BOTH, split_axis=0, concat_axis=0, tiled=True
    ).reshape(owners, cap)
    near = [box.swap(mine, "z", k) for k in range(1, nz // 2)]

    targets = jnp.concatenate([seed_self[None, :], seed_nbr.T], 0)
    names = jnp.concatenate([tgt_self[None, :] + 1, jnp.where(tgt_mask > 0, tgt_nbr + 1, 0).T], 0)
    member, line = hit_member.reshape(1, -1), hit_row.reshape(1, -1)
    holder = line // share
    code = ((holder % 2) ^ box.at["c"]) * ny + ((holder // 2) ^ box.at["y"])
    code = code * nx + ((member % nx) ^ box.at["x"])
    code = code * nz + ((member // nx) ^ box.at["z"])
    code = code * share + line % share
    hot = lax.dynamic_slice_in_dim(store, hot_local[0, 0] * BLOCK, BLOCK, 0).astype(BF16)

    def side(part):
        found = {(k, 0): box.swap(part, "x", k) for k in range(1, nx)}
        return found | {(0, k): box.swap(part, "y", k) for k in range(1, ny)}

    def corner(sides, way=0):
        found = {}
        for i in range(1, nx):
            for j in range(1, ny):
                if way:
                    found[i, j] = [box.swap(sides[i, 0], "y", j) if way == 1 else box.swap(sides[0, j], "x", i)]
                    continue
                upper, lower = jnp.split(sides[i, 0], 2)[0], jnp.split(sides[0, j], 2)[1]
                found[i, j] = [box.swap(upper, "y", j), box.swap(lower, "x", i)]
        return found

    def cached(*batches):
        pieces, bases = [], []
        for first, batch in batches:
            for (i, j), held in batch.items():
                start = first
                for piece in held if isinstance(held, list) else [held]:
                    for k in range(2):
                        pieces.append(piece if k == 0 else box.swap(piece, "c", 1))
                        bases.append(((k * ny + j) * nx + i) * nz * share + start)
                    start += piece.shape[0]
        return kernel_call(
            functools.partial(cached_body, bases=bases),
            jax.ShapeDtypeStruct((hits, wide), BF16),
        )(code, *pieces)

    far = [box.swap(mine, "z", k) for k in range(nz // 2, nz - 1)]
    home = {(0, k): cast_share(group ^ (2 * k)) for k in range(1, ny)}
    home[0, 0] = mine
    beside = {(i, k): box.swap(home[0, k], "x", i) for i in range(1, nx) for k in range(ny)}
    near, last = lax.optimization_barrier((near, mine))
    near_own = near[0] if len(near) == 1 else jnp.concatenate(near, 0)
    half = share + near_own.shape[0]
    near_side = side(near_own)
    far.append(box.swap(last, "z", nz - 1))
    asked, store_low, near_side, beside = lax.optimization_barrier(
        (asked, store_low, near_side, beside)
    )
    served = kernel_call(
        serve_body,
        jax.ShapeDtypeStruct((owners * cap, wide), BF16),
    )(asked, store_low)
    near_corner = corner(near_side, 1)
    served, far, hot, names = lax.optimization_barrier((served, far, hot, names))
    miss_rows = lax.all_to_all(
        served.reshape(owners, cap, wide), BOTH, split_axis=0, concat_axis=0, tiled=True
    ).reshape(owners * cap, wide)

    sel_hit, sel_miss, count, back, flags, code = kernel_call(
        functools.partial(tables_body, hits=hits),
        (
            jax.ShapeDtypeStruct((2, rows, hits), BF16),
            jax.ShapeDtypeStruct((2, rows, owners * cap), BF16),
            jax.ShapeDtypeStruct((rows, 1), F32),
            jax.ShapeDtypeStruct((rows, hid), BF16),
            jax.ShapeDtypeStruct((seeds, fan_two), F32),
            jax.ShapeDtypeStruct((hits, 1), I32),
        ),
    )(targets, names, slot, seed_mask.T, code, d_emb, w2_self, w2_nbr)

    far_own = jnp.concatenate(far, 0)
    far_side = side(far_own)
    first = cached((0, home), (share, {(0, 0): near_own}), (half, {(0, 0): far_own}))
    second = cached((0, beside), (share, near_side))
    far_side, near_corner, first, second = lax.optimization_barrier(
        (far_side, near_corner, first, second)
    )
    far_corner = corner(far_side)
    third = cached((half, far_side))
    far_corner, third = lax.optimization_barrier((far_corner, third))
    fourth = cached((share, near_corner), (half, far_corner))
    own_part, near_part = kernel_call(
        share_body,
        (
            jax.ShapeDtypeStruct((rows, wide), BF16),
            jax.ShapeDtypeStruct((rows, wide), F32),
        ),
    )(sel_hit, first, second, third, fourth)

    hot, own_part, near_part = lax.optimization_barrier((hot, own_part, near_part))
    far_hot = [hot] + [box.swap(hot, "y", k) for k in range(1, ny)]
    grad_scale = 1.0 / math.sqrt(seeds * owners)
    total_rows = 2 * wide + 2 * hid
    vmem, hbm = pl.BlockSpec(memory_space=pltpu.VMEM), pl.BlockSpec(memory_space=pltpu.HBM)
    streamed = (
        miss_rows, w1_self, w1_nbr, back, w2_self, w2_nbr, d_emb, sel_miss, own_part, near_part
    )
    turn = 256
    emb, *sums = pl.pallas_call(
        functools.partial(step_body, scale=grad_scale, step=turn),
        out_shape=(
            jax.ShapeDtypeStruct((seeds, hid), BF16),
            *[jax.ShapeDtypeStruct((total_rows // 4, hid), kind) for kind in (BF16,) * 4],
        ),
        in_specs=[pl.BlockSpec(memory_space=pltpu.SMEM)] + [hbm] * 10 + [vmem] * 2,
        out_specs=(vmem,) * 5,
        scratch_shapes=[pltpu.VMEM(array.shape, array.dtype) for array in streamed]
        + [
            pltpu.VMEM((rows, wide), BF16),
            pltpu.VMEM((rows, wide), BF16),
            pltpu.VMEM((rows, hid), BF16),
            pltpu.VMEM((rows, hid), BF16),
            pltpu.SemaphoreType.DMA((7 + 3 * (rows // turn),)),
        ],
        compiler_params=pltpu.CompilerParams(vmem_limit_bytes=2 * GRANT),
        cost_estimate=pl.CostEstimate(
            flops=0, bytes_accessed=0, transcendentals=0
        ),
    )(box.at["c"].reshape(1), *streamed, count, flags)
    sums, far_hot = lax.optimization_barrier((sums, far_hot))

    p, q = ([sums[2 + i], box.swap(sums[i], "c", 1)] for i in range(2))
    p, q = box.scatter((p, q), ("x", "y"))
    near_hot = [box.swap(block, "c", 1) for block in far_hot]
    p, q, near_hot = lax.optimization_barrier((p, q, near_hot))
    pairs = [join(pair, box.at["c"], BF16)[0] for pair in zip(far_hot, near_hot)]
    (new_cache,) = join(pairs, box.at["y"], F32)
    p, q = box.scatter((p, q), ("y", "x"))
    (summed,) = box.scatter((p, q), ("z", "z"), together=True)
    summed = total(summed).astype(BF16)
    p, q = box.gather(summed, "z", parts=2)
    (p,), (q,) = lax.optimization_barrier((box.gather(p, "y"), box.gather(q, "x")))
    (p,), (q,) = lax.optimization_barrier((box.gather(p, "x"), box.gather(q, "y")))
    p, q = (p, box.swap(p, "c", 1)), (q, box.swap(q, "c", 1))
    cuts = [(0, wide), (wide, 2 * wide), (2 * wide, 2 * wide + hid), (2 * wide + hid, total_rows)]
    shapes = [jax.ShapeDtypeStruct((last - at, hid), F32) for at, last in cuts]
    grads = pl.pallas_call(
        functools.partial(finish_body, cuts=cuts),
        out_shape=shapes,
        in_specs=[pl.BlockSpec(memory_space=pltpu.SMEM)] + [vmem] * 4,
        out_specs=[hbm] * 4,
        scratch_shapes=[pltpu.VMEM(x.shape, x.dtype) for x in shapes]
        + [pltpu.SemaphoreType.DMA((4,))],
        compiler_params=pltpu.CompilerParams(vmem_limit_bytes=GRANT),
    )(box.at["c"].reshape(1), *p, *q)
    return (emb, *grads, new_cache)


def solution(mesh):
    split = P(BOTH)
    in_specs = (split, P("member")) + (split,) * 11 + (P(),) * 4 + (split,)
    out_specs = (split, P(), P(), P(), P(), P("member"))
    return jax.shard_map(
        on_device, mesh=mesh, in_specs=in_specs, out_specs=out_specs, check_vma=False
    )
```

```python
import functools
import math

import jax
import jax.numpy as jnp
from jax import lax
from jax.experimental import pallas as pl
from jax.experimental.pallas import tpu as pltpu
from jax.sharding import PartitionSpec as P

BLOCK = 128
BOTH = ("group", "member")
F32, BF16, I32 = jnp.float32, jnp.bfloat16, jnp.int32
GRANT = 29 * 1024 * 1024


def dot(a, b, ca=1, cb=0):
    return lax.dot_general(a, b, (((ca,), (cb,)), ((), ())), preferred_element_type=F32)


def iota(shape, dim):
    return lax.broadcasted_iota(I32, shape, dim)


def kernel_call(body, out_shape, scratch=(), smem=0, grant=GRANT):
    def call(*operands):
        specs = [pl.BlockSpec(memory_space=pltpu.SMEM)] * smem
        specs += [pl.BlockSpec(memory_space=pltpu.VMEM)] * (len(operands) - smem)
        return pl.pallas_call(
            body,
            out_shape=out_shape,
            in_specs=specs,
            out_specs=jax.tree.map(lambda _: pl.BlockSpec(memory_space=pltpu.VMEM), out_shape),
            scratch_shapes=list(scratch),
            compiler_params=pltpu.CompilerParams(vmem_limit_bytes=grant),
            cost_estimate=pl.CostEstimate(flops=0, bytes_accessed=0, transcendentals=0),
        )(*operands)

    return call


def request_body(owner_ref, row_ref, ids_ref, slot_ref):
    count = owner_ref.shape[1]
    owners, cap = ids_ref.shape
    flags = owner_ref[...] == iota((owners, count), 0)
    flag = flags.astype(F32).astype(BF16)
    earlier = (iota((count, count), 0) < iota((count, count), 1)).astype(F32).astype(BF16)
    rank = jnp.sum(jnp.where(flags, dot(flag, earlier), 0.0), axis=0, keepdims=True).astype(I32)
    slot_ref[...] = owner_ref[...] * cap + rank
    ranked = (rank == iota((cap, count), 0)).astype(F32).astype(BF16)
    row = row_ref[...]
    high = jnp.where(flags, (row // 128).astype(F32), 0.0).astype(BF16)
    low = jnp.where(flags, (row % 128).astype(F32), 0.0).astype(BF16)
    ids_ref[...] = (dot(high, ranked, 1, 1) * 128.0 + dot(low, ranked, 1, 1)).astype(I32)


def serve_body(ids_ref, store_ref, rows_ref):
    peers, cap = ids_ref.shape
    total, held = peers * cap, store_ref.shape[0]
    ids = ids_ref[...]
    spread = (iota((total, peers), 0) // cap == iota((total, peers), 1)).astype(F32).astype(BF16)
    high = dot(spread, (ids // 128).astype(F32).astype(BF16))
    low = dot(spread, (ids % 128).astype(F32).astype(BF16))
    here = iota((total, cap), 0) % cap == iota((total, cap), 1)
    flat = jnp.sum(jnp.where(here, high * 128.0 + low, 0.0), axis=1, keepdims=True).astype(I32)
    step = 256
    for at in range(0, total, step):
        pick = (flat[at : at + step] == iota((step, held), 1)).astype(F32).astype(BF16)
        rows_ref[at : at + step, :] = dot(pick, store_ref[...]).astype(BF16)


def tables_body(
    targets_ref, names_ref, slot_ref, mask_ref, code_ref, emb_ref, w2s_ref, w2n_ref,
    sel_hit_ref, sel_miss_ref, count_ref, back_ref, flag_ref, column_ref, *, hits,
):
    seeds, total = targets_ref.shape[1], names_ref.shape[1]
    misses = slot_ref.shape[1]
    slots = sel_miss_ref.shape[2]
    fan, fan_two = names_ref.shape[0] - 1, mask_ref.shape[0]
    one, zero = jnp.array(1, BF16), jnp.array(0, BF16)

    def columns(rows):
        rows = rows.astype(F32)
        pad = jnp.zeros((-rows.shape[0] % 8, rows.shape[1]), F32)
        return jnp.concatenate([rows, pad], 0).T if pad.shape[0] else rows.T

    column_ref[...] = columns(code_ref[...])[:, 0:1].astype(I32)
    names = names_ref[...]
    high = (names // 128).astype(F32).astype(BF16)
    low = (names % 128).astype(F32).astype(BF16)
    place = (slot_ref[...] == iota((slots, misses), 0)).astype(F32).astype(BF16)
    targets = columns(targets_ref[...]).astype(I32)
    for turn in range(fan_two + 1):
        cut = slice(turn * seeds, (turn + 1) * seeds)
        pick = (targets[:, turn : turn + 1] == iota((seeds, total), 1)).astype(F32).astype(BF16)
        named = (dot(pick, high, 1, 1) * 128.0 + dot(pick, low, 1, 1)).astype(I32) - 1
        here = named[:, 1:] >= 0
        count_ref[cut, :] = jnp.maximum(jnp.sum(here.astype(F32), axis=1, keepdims=True), 1.0)
        for first, width in ((0, hits), (hits, misses)):
            lane = (iota((seeds, width), 1) + first).astype(jnp.int16)
            own = jnp.where(named[:, 0:1].astype(jnp.int16) == lane, one, zero)
            near = jnp.zeros((seeds, width), BF16)
            for k in range(1, fan + 1):
                near = near + jnp.where(named[:, k : k + 1].astype(jnp.int16) == lane, one, zero)
            if first == 0:
                sel_hit_ref[0, cut, :] = own
                sel_hit_ref[1, cut, :] = near
            else:
                sel_miss_ref[0, cut, :] = dot(own, place, 1, 1).astype(BF16)
                sel_miss_ref[1, cut, :] = dot(near, place, 1, 1).astype(BF16)
    mask = columns(mask_ref[...])[:, :fan_two]
    flag_ref[...] = mask
    count_two = jnp.maximum(jnp.sum(mask, axis=1, keepdims=True), 1.0)
    back_ref[0:seeds, :] = dot(emb_ref[...], w2s_ref[...], 1, 1).astype(BF16)
    back_mean = (dot(emb_ref[...], w2n_ref[...], 1, 1) / count_two).astype(BF16).astype(F32)
    for k in range(fan_two):
        at = (k + 1) * seeds
        back_ref[at : at + seeds, :] = (mask[:, k : k + 1] * back_mean).astype(BF16)


def cached_body(code_ref, *refs, bases):
    pieces, held_ref = refs[:-1], refs[-1]
    step = 512
    groups, depth = [], step
    for i, piece in enumerate(pieces):
        if depth + piece.shape[0] > 512:
            groups, depth = groups + [[]], 0
        groups[-1].append(i)
        depth += piece.shape[0]

    @pl.loop(0, code_ref.shape[0] // step)
    def _(turn):
        cut = pl.ds(pl.multiple_of(turn * step, step), step)
        total = None
        for group in groups:
            lanes = [iota((step, pieces[i].shape[0]), 1) + bases[i] for i in group]
            lane = lanes[0] if len(group) == 1 else jnp.concatenate(lanes, 1)
            rows = [pieces[i][...] for i in group]
            pick = (code_ref[cut, :] == lane).astype(F32).astype(BF16)
            part = dot(pick, rows[0] if len(group) == 1 else jnp.concatenate(rows, 0))
            total = part if total is None else total + part
        held_ref[cut, :] = total.astype(BF16)


def share_body(sel_ref, *refs):
    parts, (own_ref, near_ref) = refs[:-2], refs[-2:]
    held = parts[0][...]
    for part in parts[1:]:
        held = held + part[...]
    step = 256
    for at in range(0, own_ref.shape[0], step):
        own_ref[at : at + step, :] = dot(sel_ref[0, at : at + step, :], held).astype(BF16)
        near_ref[at : at + step, :] = dot(sel_ref[1, at : at + step, :], held)


def join_body(me_ref, *refs, count, parts):
    pieces, outs = refs[:count], refs[count:]
    for k in range(count):
        depth = pieces[k].shape[0] // parts
        place = pl.multiple_of((me_ref[0] ^ k) * depth, 16)
        for j in range(parts):
            value = pieces[k][j * depth : (j + 1) * depth, :]
            outs[j][pl.ds(place, depth), :] = value.astype(outs[j].dtype)


def join(pieces, me, dtype, parts=1):
    count = len(pieces)
    depth, width = pieces[0].shape[0] // parts, pieces[0].shape[1]
    if depth % 16 == 0:
        return kernel_call(
            functools.partial(join_body, count=count, parts=parts),
            [jax.ShapeDtypeStruct((count * depth, width), dtype)] * parts,
            smem=1,
        )(me.reshape(1), *pieces)
    outs = [jnp.zeros((count * depth, width), dtype)] * parts
    for k in range(count):
        for j in range(parts):
            value = pieces[k][j * depth : (j + 1) * depth].astype(dtype)
            outs[j] = lax.dynamic_update_slice_in_dim(outs[j], value, (me ^ k) * depth, 0)
    return outs


def step_body(core_ref, *refs, scale, step):
    sources, (count_ref, mask_ref, out_ref, *refs) = refs[:10], refs[10:]
    send_refs, keep_refs, refs = refs[:2], refs[2:4], refs[4:]
    held, (self_ref, mean_ref, hid_ref, bp_ref, sems) = refs[:10], refs[10:]
    miss_ref, w1s_ref, w1n_ref, back_ref, w2s_ref, w2n_ref, emb_ref, *turned = held
    sel_ref, own_ref, near_ref = turned
    rows, wide = own_ref.shape
    seeds = mask_ref.shape[0]
    hid = w1s_ref.shape[1]
    turns = rows // step

    def copy(i, turn=None):
        source, target, number = sources[i], held[i], i
        if turn is not None:
            cut = slice(turn * step, (turn + 1) * step)
            source, target = (
                (ref.at[:, cut, :] if len(ref.shape) == 3 else ref.at[cut, :])
                for ref in (source, target)
            )
            number = 7 + (i - 7) * turns + turn
        return pltpu.make_async_copy(source, target, sems.at[number])

    order = [(0,), (7, 0), (8, 0), (9, 0), (1,), (2,), (3,)]
    order += [(i, turn) for turn in range(1, turns) for i in (7, 8, 9)] + [(4,), (5,), (6,)]
    for item in order:
        copy(*item).start()
    copy(0).wait()
    for turn in range(turns):
        cut = slice(turn * step, (turn + 1) * step)
        copy(7, turn).wait()
        own = dot(sel_ref[0, cut, :], miss_ref[...])
        near = dot(sel_ref[1, cut, :], miss_ref[...])
        copy(8, turn).wait()
        copy(9, turn).wait()
        own = (own_ref[cut, :].astype(F32) + own).astype(BF16)
        mean = ((near_ref[cut, :] + near) / count_ref[cut, :]).astype(BF16)
        self_ref[cut, :] = own
        mean_ref[cut, :] = mean
        if turn == 0:
            copy(1).wait()
            copy(2).wait()
        pre = dot(own, w1s_ref[...]) + dot(mean, w1n_ref[...])
        gate = jax.nn.sigmoid(pre)
        hid_ref[cut, :] = (pre * gate).astype(BF16)
        slope = gate * (1.0 + pre * (1.0 - gate))
        if turn == 0:
            copy(3).wait()
        bp_ref[cut, :] = (back_ref[cut, :].astype(F32) * slope).astype(BF16)

    core = core_ref[0]
    quarter = keep_refs[0].shape[0]

    def put(at, value):
        value = value * scale
        first = 0
        while first < value.shape[0]:
            number, place = (at + first) // quarter, (at + first) % quarter
            depth = min(value.shape[0] - first, quarter - place)
            part, rows_at = value[first : first + depth], slice(place, place + depth)

            @pl.when(core == number // 2)
            def _(part=part, rows_at=rows_at, ref=keep_refs[number % 2]):
                ref[rows_at, :] = part.astype(BF16)

            @pl.when(core != number // 2)
            def _(part=part, rows_at=rows_at, ref=send_refs[number % 2]):
                ref[rows_at, :] = part.astype(BF16)

            first += depth

    mask = mask_ref[...]
    count_two = jnp.maximum(jnp.sum(mask, axis=1, keepdims=True), 1.0)
    total = jnp.zeros((seeds, hid), F32)
    for k in range(mask.shape[1]):
        at = (k + 1) * seeds
        total = total + mask[:, k : k + 1] * hid_ref[at : at + seeds, :].astype(F32)
    mean_two = (total / count_two).astype(BF16)
    self_two = hid_ref[0:seeds, :]
    for i in (4, 5, 6):
        copy(i).wait()
    out_ref[...] = (dot(self_two, w2s_ref[...]) + dot(mean_two, w2n_ref[...])).astype(BF16)
    put(2 * wide, dot(self_two, emb_ref[...], 0, 0))
    put(2 * wide + hid, dot(mean_two, emb_ref[...], 0, 0))
    for base, ref in ((0, self_ref), (wide, mean_ref)):
        for at in range(0, wide, step):
            put(base + at, dot(ref[:, at : at + step], bp_ref[...], 0, 0))


def fold_body(me_ref, *refs, terms, counts, together):
    ins, outs = refs[: sum(terms)], refs[sum(terms) :]
    for i, count in enumerate(counts):
        held, ins = ins[: terms[i]], ins[terms[i] :]
        depth = held[0].shape[0] // count
        for k in range(count):
            place = pl.ds(pl.multiple_of((me_ref[i] ^ k) * depth, 16), depth)
            value = held[0][place, :].astype(F32)
            for term in held[1:]:
                value = value + term[place, :].astype(F32)
            if together:
                outs[k][i * depth : (i + 1) * depth, :] = value.astype(outs[k].dtype)
            else:
                outs[k][...] = value.astype(outs[k].dtype)
        if not together:
            outs = outs[count:]


def fold(chains, counts, me, together):
    width = chains[0][0].shape[1]
    depths = [chain[0].shape[0] // count for chain, count in zip(chains, counts)]
    if all(depth % 16 == 0 for depth in depths):
        groups = [(sum(depths), counts[0])] if together else list(zip(depths, counts))
        shapes = [
            jax.ShapeDtypeStruct((depth, width), BF16 if k else F32)
            for depth, count in groups
            for k in range(count)
        ]
        out = iter(kernel_call(
            functools.partial(
                fold_body, terms=[len(c) for c in chains], counts=counts, together=together
            ),
            shapes,
            smem=1,
        )(jnp.stack(me), *[term for chain in chains for term in chain]))
        return [[next(out) for _ in range(count)] for _, count in groups]
    found = []
    for chain, count, depth, at in zip(chains, counts, depths, me):
        parts = [
            total([lax.dynamic_slice_in_dim(t, (at ^ k) * depth, depth, 0) for t in chain])
            for k in range(count)
        ]
        found.append([part.astype(BF16) if k else part for k, part in enumerate(parts)])
    return [[jnp.concatenate(pair, 0) for pair in zip(*found)]] if together else found


def finish_body(core_ref, *refs, cuts):
    (p, p_far, q, q_far), outs, held, sems = refs[:4], refs[4:8], refs[8:12], refs[12]
    quarter = p.shape[0]
    for near_core in range(2):

        @pl.when(core_ref[0] == near_core)
        def _():
            order = [(p, p_far), (q, q_far)]
            order = [pair[core != near_core] for core in range(2) for pair in order]
            for i, (first, last) in enumerate(cuts):
                at = first
                while at < last:
                    number, place = at // quarter, at % quarter
                    upto = min(last, (number + 1) * quarter)
                    held[i][at - first : upto - first, :] = order[number][
                        place : place + upto - at, :
                    ].astype(F32)
                    at = upto
                pltpu.make_async_copy(held[i], outs[i], sems.at[i]).start()

    for i in range(len(cuts)):
        pltpu.make_async_copy(held[i], outs[i], sems.at[i]).wait()


class Slice:
    def __init__(self):
        self.groups, self.members = lax.axis_size("group"), lax.axis_size("member")
        self.size = {"c": 2, "y": self.groups // 2, "z": 4, "x": self.members // 4}
        group, member = lax.axis_index("group"), lax.axis_index("member")
        self.at = {
            "c": group % 2,
            "y": group // 2,
            "z": member // self.size["x"],
            "x": member % self.size["x"],
        }

    def swap(self, array, axis, k):
        stride = {"c": 1, "y": 2, "z": self.size["x"], "x": 1}[axis]
        name, count = ("group", self.groups) if axis in "cy" else ("member", self.members)
        return lax.ppermute(array, name, [(i, i ^ (k * stride)) for i in range(count)])

    def scatter(self, chains, axes, together=False):
        out = fold(chains, [self.size[a] for a in axes], [self.at[a] for a in axes], together)
        if together:
            axes = axes[:1]
        return [
            [mine] + [self.swap(part, axis, k + 1) for k, part in enumerate(parts)]
            for (mine, *parts), axis in zip(out, axes)
        ]

    def gather(self, part, axis, dtype=BF16, parts=1):
        pieces = [part] + [self.swap(part, axis, k) for k in range(1, self.size[axis])]
        return join(pieces, self.at[axis], dtype, parts)


def total(terms):
    out = terms[0].astype(F32)
    for term in terms[1:]:
        out = out + term.astype(F32)
    return out


def on_device(
    store,
    cache,
    hot_local,
    hit_member,
    hit_row,
    miss_owner,
    miss_row,
    tgt_self,
    tgt_nbr,
    tgt_mask,
    seed_self,
    seed_nbr,
    seed_mask,
    w1_self,
    w1_nbr,
    w2_self,
    w2_nbr,
    d_emb,
):
    box = Slice()
    nx, ny, nz = box.size["x"], box.size["y"], box.size["z"]
    wide, hid = w1_self.shape
    owners = box.groups * box.members
    hits, misses = hit_row.shape[0], miss_row.shape[0]
    cap = 2 * misses // owners
    seeds, fan_two = seed_nbr.shape
    rows = seeds * (fan_two + 1)

    share = cache.shape[0] // box.groups
    group = lax.axis_index("group")

    def cast_share(number):
        return lax.dynamic_slice_in_dim(cache, number * share, share, 0).astype(BF16)

    mine = cast_share(group)

    ids, slot = kernel_call(
        request_body,
        (
            jax.ShapeDtypeStruct((owners, cap), I32),
            jax.ShapeDtypeStruct((1, misses), I32),
        ),
    )(miss_owner.reshape(1, -1), miss_row.reshape(1, -1))
    store_low = store.astype(BF16)
    asked = lax.all_to_all(
        ids.reshape(owners, 1, cap), BOTH, split_axis=0, concat_axis=0, tiled=True
    ).reshape(owners, cap)
    near = [box.swap(mine, "z", k) for k in range(1, nz // 2)]

    targets = jnp.concatenate([seed_self[None, :], seed_nbr.T], 0)
    names = jnp.concatenate([tgt_self[None, :] + 1, jnp.where(tgt_mask > 0, tgt_nbr + 1, 0).T], 0)
    member, line = hit_member.reshape(1, -1), hit_row.reshape(1, -1)
    holder = line // share
    code = ((holder % 2) ^ box.at["c"]) * ny + ((holder // 2) ^ box.at["y"])
    code = code * nx + ((member % nx) ^ box.at["x"])
    code = code * nz + ((member // nx) ^ box.at["z"])
    code = code * share + line % share
    hot = lax.dynamic_slice_in_dim(store, hot_local[0, 0] * BLOCK, BLOCK, 0).astype(BF16)

    def side(part):
        found = {(k, 0): box.swap(part, "x", k) for k in range(1, nx)}
        return found | {(0, k): box.swap(part, "y", k) for k in range(1, ny)}

    def corner(sides, way=0):
        found = {}
        for i in range(1, nx):
            for j in range(1, ny):
                if way:
                    found[i, j] = [box.swap(sides[i, 0], "y", j) if way == 1 else box.swap(sides[0, j], "x", i)]
                    continue
                upper, lower = jnp.split(sides[i, 0], 2)[0], jnp.split(sides[0, j], 2)[1]
                found[i, j] = [box.swap(upper, "y", j), box.swap(lower, "x", i)]
        return found

    def cached(*batches):
        pieces, bases = [], []
        for first, batch in batches:
            for (i, j), held in batch.items():
                start = first
                for piece in held if isinstance(held, list) else [held]:
                    for k in range(2):
                        pieces.append(piece if k == 0 else box.swap(piece, "c", 1))
                        bases.append(((k * ny + j) * nx + i) * nz * share + start)
                    start += piece.shape[0]
        return kernel_call(
            functools.partial(cached_body, bases=bases),
            jax.ShapeDtypeStruct((hits, wide), BF16),
        )(code, *pieces)

    far = [box.swap(mine, "z", k) for k in range(nz // 2, nz - 1)]
    home = {(0, k): cast_share(group ^ (2 * k)) for k in range(1, ny)}
    home[0, 0] = mine
    beside = {(i, k): box.swap(home[0, k], "x", i) for i in range(1, nx) for k in range(ny)}
    near, last = lax.optimization_barrier((near, mine))
    near_own = near[0] if len(near) == 1 else jnp.concatenate(near, 0)
    half = share + near_own.shape[0]
    near_side = side(near_own)
    far.append(box.swap(last, "z", nz - 1))
    asked, store_low, near_side, beside = lax.optimization_barrier(
        (asked, store_low, near_side, beside)
    )
    served = kernel_call(
        serve_body,
        jax.ShapeDtypeStruct((owners * cap, wide), BF16),
    )(asked, store_low)
    near_corner = corner(near_side, 1)
    served, far, hot, names = lax.optimization_barrier((served, far, hot, names))
    miss_rows = lax.all_to_all(
        served.reshape(owners, cap, wide), BOTH, split_axis=0, concat_axis=0, tiled=True
    ).reshape(owners * cap, wide)

    sel_hit, sel_miss, count, back, flags, code = kernel_call(
        functools.partial(tables_body, hits=hits),
        (
            jax.ShapeDtypeStruct((2, rows, hits), BF16),
            jax.ShapeDtypeStruct((2, rows, owners * cap), BF16),
            jax.ShapeDtypeStruct((rows, 1), F32),
            jax.ShapeDtypeStruct((rows, hid), BF16),
            jax.ShapeDtypeStruct((seeds, fan_two), F32),
            jax.ShapeDtypeStruct((hits, 1), I32),
        ),
    )(targets, names, slot, seed_mask.T, code, d_emb, w2_self, w2_nbr)

    far_own = jnp.concatenate(far, 0)
    far_side = side(far_own)
    first = cached((0, home), (share, {(0, 0): near_own}), (half, {(0, 0): far_own}))
    second = cached((0, beside), (share, near_side))
    far_side, near_corner, first, second = lax.optimization_barrier(
        (far_side, near_corner, first, second)
    )
    far_corner = corner(far_side)
    third = cached((half, far_side))
    far_corner, third = lax.optimization_barrier((far_corner, third))
    fourth = cached((share, near_corner), (half, far_corner))
    own_part, near_part = kernel_call(
        share_body,
        (
            jax.ShapeDtypeStruct((rows, wide), BF16),
            jax.ShapeDtypeStruct((rows, wide), F32),
        ),
    )(sel_hit, first, second, third, fourth)

    hot, own_part, near_part = lax.optimization_barrier((hot, own_part, near_part))
    far_hot = [hot] + [box.swap(hot, "y", k) for k in range(1, ny)]
    grad_scale = 1.0 / math.sqrt(seeds * owners)
    total_rows = 2 * wide + 2 * hid
    vmem, hbm = pl.BlockSpec(memory_space=pltpu.VMEM), pl.BlockSpec(memory_space=pltpu.HBM)
    streamed = (
        miss_rows, w1_self, w1_nbr, back, w2_self, w2_nbr, d_emb, sel_miss, own_part, near_part
    )
    turn = 384
    emb, *sums = pl.pallas_call(
        functools.partial(step_body, scale=grad_scale, step=turn),
        out_shape=(
            jax.ShapeDtypeStruct((seeds, hid), BF16),
            *[jax.ShapeDtypeStruct((total_rows // 4, hid), kind) for kind in (BF16,) * 4],
        ),
        in_specs=[pl.BlockSpec(memory_space=pltpu.SMEM)] + [hbm] * 10 + [vmem] * 2,
        out_specs=(vmem,) * 5,
        scratch_shapes=[pltpu.VMEM(array.shape, array.dtype) for array in streamed]
        + [
            pltpu.VMEM((rows, wide), BF16),
            pltpu.VMEM((rows, wide), BF16),
            pltpu.VMEM((rows, hid), BF16),
            pltpu.VMEM((rows, hid), BF16),
            pltpu.SemaphoreType.DMA((7 + 3 * (rows // turn),)),
        ],
        compiler_params=pltpu.CompilerParams(vmem_limit_bytes=2 * GRANT),
        cost_estimate=pl.CostEstimate(
            flops=0, bytes_accessed=0, transcendentals=0
        ),
    )(box.at["c"].reshape(1), *streamed, count, flags)
    sums, far_hot = lax.optimization_barrier((sums, far_hot))

    p, q = ([sums[2 + i].astype(F32), box.swap(sums[i], "c", 1)] for i in range(2))
    p, q = box.scatter((p, q), ("x", "y"))
    near_hot = [box.swap(block, "c", 1) for block in far_hot]
    p, q, near_hot = lax.optimization_barrier((p, q, near_hot))
    pairs = [join(pair, box.at["c"], BF16)[0] for pair in zip(far_hot, near_hot)]
    (new_cache,) = join(pairs, box.at["y"], F32)
    p, q = box.scatter((p, q), ("y", "x"))
    (summed,) = box.scatter((p, q), ("z", "z"), together=True)
    summed = total(summed).astype(BF16)
    p, q = box.gather(summed, "z", parts=2)
    (p,), (q,) = lax.optimization_barrier((box.gather(p, "y"), box.gather(q, "x")))
    (p,), (q,) = lax.optimization_barrier((box.gather(p, "x"), box.gather(q, "y")))
    p, q = (p, box.swap(p, "c", 1)), (q, box.swap(q, "c", 1))
    cuts = [(0, wide), (wide, 2 * wide), (2 * wide, 2 * wide + hid), (2 * wide + hid, total_rows)]
    shapes = [jax.ShapeDtypeStruct((last - at, hid), F32) for at, last in cuts]
    grads = pl.pallas_call(
        functools.partial(finish_body, cuts=cuts),
        out_shape=shapes,
        in_specs=[pl.BlockSpec(memory_space=pltpu.SMEM)] + [vmem] * 4,
        out_specs=[hbm] * 4,
        scratch_shapes=[pltpu.VMEM(x.shape, x.dtype) for x in shapes]
        + [pltpu.SemaphoreType.DMA((4,))],
        compiler_params=pltpu.CompilerParams(vmem_limit_bytes=GRANT),
    )(box.at["c"].reshape(1), *p, *q)
    return (emb, *grads, new_cache)


def solution(mesh):
    split = P(BOTH)
    in_specs = (split, P("member")) + (split,) * 11 + (P(),) * 4 + (split,)
    out_specs = (split, P(), P(), P(), P(), P("member"))
    return jax.shard_map(
        on_device, mesh=mesh, in_specs=in_specs, out_specs=out_specs, check_vma=False
    )
```

```python
import functools
import math

import jax
import jax.numpy as jnp
from jax import lax
from jax.experimental import pallas as pl
from jax.experimental.pallas import tpu as pltpu
from jax.sharding import PartitionSpec as P

BLOCK = 128
BOTH = ("group", "member")
F32, BF16, I32 = jnp.float32, jnp.bfloat16, jnp.int32
GRANT = 29 * 1024 * 1024


def dot(a, b, ca=1, cb=0):
    return lax.dot_general(a, b, (((ca,), (cb,)), ((), ())), preferred_element_type=F32)


def iota(shape, dim):
    return lax.broadcasted_iota(I32, shape, dim)


def kernel_call(body, out_shape, scratch=(), smem=0, grant=GRANT):
    def call(*operands):
        specs = [pl.BlockSpec(memory_space=pltpu.SMEM)] * smem
        specs += [pl.BlockSpec(memory_space=pltpu.VMEM)] * (len(operands) - smem)
        return pl.pallas_call(
            body,
            out_shape=out_shape,
            in_specs=specs,
            out_specs=jax.tree.map(lambda _: pl.BlockSpec(memory_space=pltpu.VMEM), out_shape),
            scratch_shapes=list(scratch),
            compiler_params=pltpu.CompilerParams(vmem_limit_bytes=grant),
            cost_estimate=pl.CostEstimate(flops=0, bytes_accessed=0, transcendentals=0),
        )(*operands)

    return call


def request_body(owner_ref, row_ref, ids_ref, slot_ref):
    count = owner_ref.shape[1]
    owners, cap = ids_ref.shape
    flags = owner_ref[...] == iota((owners, count), 0)
    flag = flags.astype(F32).astype(BF16)
    earlier = (iota((count, count), 0) < iota((count, count), 1)).astype(F32).astype(BF16)
    rank = jnp.sum(jnp.where(flags, dot(flag, earlier), 0.0), axis=0, keepdims=True).astype(I32)
    slot_ref[...] = owner_ref[...] * cap + rank
    ranked = (rank == iota((cap, count), 0)).astype(F32).astype(BF16)
    row = row_ref[...]
    high = jnp.where(flags, (row // 128).astype(F32), 0.0).astype(BF16)
    low = jnp.where(flags, (row % 128).astype(F32), 0.0).astype(BF16)
    ids_ref[...] = (dot(high, ranked, 1, 1) * 128.0 + dot(low, ranked, 1, 1)).astype(I32)


def serve_body(ids_ref, store_ref, rows_ref):
    peers, cap = ids_ref.shape
    total, held = peers * cap, store_ref.shape[0]
    ids = ids_ref[...]
    spread = (iota((total, peers), 0) // cap == iota((total, peers), 1)).astype(F32).astype(BF16)
    high = dot(spread, (ids // 128).astype(F32).astype(BF16))
    low = dot(spread, (ids % 128).astype(F32).astype(BF16))
    here = iota((total, cap), 0) % cap == iota((total, cap), 1)
    flat = jnp.sum(jnp.where(here, high * 128.0 + low, 0.0), axis=1, keepdims=True).astype(I32)
    step = 256
    for at in range(0, total, step):
        pick = (flat[at : at + step] == iota((step, held), 1)).astype(F32).astype(BF16)
        rows_ref[at : at + step, :] = dot(pick, store_ref[...]).astype(BF16)


def tables_body(
    targets_ref, names_ref, slot_ref, mask_ref, code_ref, emb_ref, w2s_ref, w2n_ref,
    sel_hit_ref, sel_miss_ref, count_ref, back_ref, flag_ref, column_ref, *, hits,
):
    seeds, total = targets_ref.shape[1], names_ref.shape[1]
    misses = slot_ref.shape[1]
    slots = sel_miss_ref.shape[2]
    fan, fan_two = names_ref.shape[0] - 1, mask_ref.shape[0]
    one, zero = jnp.array(1, BF16), jnp.array(0, BF16)

    def columns(rows):
        rows = rows.astype(F32)
        pad = jnp.zeros((-rows.shape[0] % 8, rows.shape[1]), F32)
        return jnp.concatenate([rows, pad], 0).T if pad.shape[0] else rows.T

    column_ref[...] = columns(code_ref[...])[:, 0:1].astype(I32)
    names = names_ref[...]
    high = (names // 128).astype(F32).astype(BF16)
    low = (names % 128).astype(F32).astype(BF16)
    place = (slot_ref[...] == iota((slots, misses), 0)).astype(F32).astype(BF16)
    targets = columns(targets_ref[...]).astype(I32)
    for turn in range(fan_two + 1):
        cut = slice(turn * seeds, (turn + 1) * seeds)
        pick = (targets[:, turn : turn + 1] == iota((seeds, total), 1)).astype(F32).astype(BF16)
        named = (dot(pick, high, 1, 1) * 128.0 + dot(pick, low, 1, 1)).astype(I32) - 1
        here = named[:, 1:] >= 0
        count_ref[cut, :] = jnp.maximum(jnp.sum(here.astype(F32), axis=1, keepdims=True), 1.0)
        for first, width in ((0, hits), (hits, misses)):
            lane = (iota((seeds, width), 1) + first).astype(jnp.int16)
            own = jnp.where(named[:, 0:1].astype(jnp.int16) == lane, one, zero)
            near = jnp.zeros((seeds, width), BF16)
            for k in range(1, fan + 1):
                near = near + jnp.where(named[:, k : k + 1].astype(jnp.int16) == lane, one, zero)
            if first == 0:
                sel_hit_ref[0, cut, :] = own
                sel_hit_ref[1, cut, :] = near
            else:
                sel_miss_ref[0, cut, :] = dot(own, place, 1, 1).astype(BF16)
                sel_miss_ref[1, cut, :] = dot(near, place, 1, 1).astype(BF16)
    mask = columns(mask_ref[...])[:, :fan_two]
    flag_ref[...] = mask
    count_two = jnp.maximum(jnp.sum(mask, axis=1, keepdims=True), 1.0)
    back_ref[0:seeds, :] = dot(emb_ref[...], w2s_ref[...], 1, 1).astype(BF16)
    back_mean = (dot(emb_ref[...], w2n_ref[...], 1, 1) / count_two).astype(BF16).astype(F32)
    for k in range(fan_two):
        at = (k + 1) * seeds
        back_ref[at : at + seeds, :] = (mask[:, k : k + 1] * back_mean).astype(BF16)


def cached_body(code_ref, *refs, bases):
    pieces, held_ref = refs[:-1], refs[-1]
    step = 512
    groups, depth = [], step
    for i, piece in enumerate(pieces):
        if depth + piece.shape[0] > 512:
            groups, depth = groups + [[]], 0
        groups[-1].append(i)
        depth += piece.shape[0]

    @pl.loop(0, code_ref.shape[0] // step)
    def _(turn):
        cut = pl.ds(pl.multiple_of(turn * step, step), step)
        total = None
        for group in groups:
            lanes = [iota((step, pieces[i].shape[0]), 1) + bases[i] for i in group]
            lane = lanes[0] if len(group) == 1 else jnp.concatenate(lanes, 1)
            rows = [pieces[i][...] for i in group]
            pick = (code_ref[cut, :] == lane).astype(F32).astype(BF16)
            part = dot(pick, rows[0] if len(group) == 1 else jnp.concatenate(rows, 0))
            total = part if total is None else total + part
        held_ref[cut, :] = total.astype(BF16)


def share_body(sel_ref, *refs):
    parts, (own_ref, near_ref) = refs[:-2], refs[-2:]
    held = parts[0][...]
    for part in parts[1:]:
        held = held + part[...]
    step = 256
    for at in range(0, own_ref.shape[0], step):
        own_ref[at : at + step, :] = dot(sel_ref[0, at : at + step, :], held).astype(BF16)
        near_ref[at : at + step, :] = dot(sel_ref[1, at : at + step, :], held)


def join_body(me_ref, *refs, count, parts):
    pieces, outs = refs[:count], refs[count:]
    for k in range(count):
        depth = pieces[k].shape[0] // parts
        place = pl.multiple_of((me_ref[0] ^ k) * depth, 16)
        for j in range(parts):
            value = pieces[k][j * depth : (j + 1) * depth, :]
            outs[j][pl.ds(place, depth), :] = value.astype(outs[j].dtype)


def join(pieces, me, dtype, parts=1):
    count = len(pieces)
    depth, width = pieces[0].shape[0] // parts, pieces[0].shape[1]
    if depth % 16 == 0:
        return kernel_call(
            functools.partial(join_body, count=count, parts=parts),
            [jax.ShapeDtypeStruct((count * depth, width), dtype)] * parts,
            smem=1,
        )(me.reshape(1), *pieces)
    outs = [jnp.zeros((count * depth, width), dtype)] * parts
    for k in range(count):
        for j in range(parts):
            value = pieces[k][j * depth : (j + 1) * depth].astype(dtype)
            outs[j] = lax.dynamic_update_slice_in_dim(outs[j], value, (me ^ k) * depth, 0)
    return outs


def step_body(core_ref, *refs, scale, step):
    sources, (count_ref, mask_ref, out_ref, *refs) = refs[:10], refs[10:]
    send_refs, keep_refs, refs = refs[:2], refs[2:4], refs[4:]
    held, (self_ref, mean_ref, hid_ref, bp_ref, sems) = refs[:10], refs[10:]
    miss_ref, w1s_ref, w1n_ref, back_ref, w2s_ref, w2n_ref, emb_ref, *turned = held
    sel_ref, own_ref, near_ref = turned
    rows, wide = own_ref.shape
    seeds = mask_ref.shape[0]
    hid = w1s_ref.shape[1]
    turns = rows // step

    def copy(i, turn=None):
        source, target, number = sources[i], held[i], i
        if turn is not None:
            cut = slice(turn * step, (turn + 1) * step)
            source, target = (
                (ref.at[:, cut, :] if len(ref.shape) == 3 else ref.at[cut, :])
                for ref in (source, target)
            )
            number = 7 + (i - 7) * turns + turn
        return pltpu.make_async_copy(source, target, sems.at[number])

    order = [(0,), (7, 0), (8, 0), (9, 0), (1,), (2,), (3,)]
    order += [(i, turn) for turn in range(1, turns) for i in (7, 8, 9)] + [(4,), (5,), (6,)]
    for item in order:
        copy(*item).start()
    copy(0).wait()
    for turn in range(turns):
        cut = slice(turn * step, (turn + 1) * step)
        copy(7, turn).wait()
        own = dot(sel_ref[0, cut, :], miss_ref[...])
        near = dot(sel_ref[1, cut, :], miss_ref[...])
        copy(8, turn).wait()
        copy(9, turn).wait()
        own = (own_ref[cut, :].astype(F32) + own).astype(BF16)
        mean = ((near_ref[cut, :] + near) / count_ref[cut, :]).astype(BF16)
        self_ref[cut, :] = own
        mean_ref[cut, :] = mean
        if turn == 0:
            copy(1).wait()
            copy(2).wait()
        pre = dot(own, w1s_ref[...]) + dot(mean, w1n_ref[...])
        gate = jax.nn.sigmoid(pre)
        hid_ref[cut, :] = (pre * gate).astype(BF16)
        slope = gate * (1.0 + pre * (1.0 - gate))
        if turn == 0:
            copy(3).wait()
        bp_ref[cut, :] = (back_ref[cut, :].astype(F32) * slope).astype(BF16)

    core = core_ref[0]
    quarter = keep_refs[0].shape[0]

    def put(at, value):
        value = value * scale
        first = 0
        while first < value.shape[0]:
            number, place = (at + first) // quarter, (at + first) % quarter
            depth = min(value.shape[0] - first, quarter - place)
            part, rows_at = value[first : first + depth], slice(place, place + depth)

            @pl.when(core == number // 2)
            def _(part=part, rows_at=rows_at, ref=keep_refs[number % 2]):
                ref[rows_at, :] = part.astype(BF16)

            @pl.when(core != number // 2)
            def _(part=part, rows_at=rows_at, ref=send_refs[number % 2]):
                ref[rows_at, :] = part.astype(BF16)

            first += depth

    mask = mask_ref[...]
    count_two = jnp.maximum(jnp.sum(mask, axis=1, keepdims=True), 1.0)
    total = jnp.zeros((seeds, hid), F32)
    for k in range(mask.shape[1]):
        at = (k + 1) * seeds
        total = total + mask[:, k : k + 1] * hid_ref[at : at + seeds, :].astype(F32)
    mean_two = (total / count_two).astype(BF16)
    self_two = hid_ref[0:seeds, :]
    for i in (4, 5, 6):
        copy(i).wait()
    out_ref[...] = (dot(self_two, w2s_ref[...]) + dot(mean_two, w2n_ref[...])).astype(BF16)
    put(2 * wide, dot(self_two, emb_ref[...], 0, 0))
    put(2 * wide + hid, dot(mean_two, emb_ref[...], 0, 0))
    for base, ref in ((0, self_ref), (wide, mean_ref)):
        for at in range(0, wide, step):
            put(base + at, dot(ref[:, at : at + step], bp_ref[...], 0, 0))


def fold_body(me_ref, *refs, terms, counts, together):
    ins, outs = refs[: sum(terms)], refs[sum(terms) :]
    for i, count in enumerate(counts):
        held, ins = ins[: terms[i]], ins[terms[i] :]
        depth = held[0].shape[0] // count
        for k in range(count):
            place = pl.ds(pl.multiple_of((me_ref[i] ^ k) * depth, 16), depth)
            value = held[0][place, :].astype(F32)
            for term in held[1:]:
                value = value + term[place, :].astype(F32)
            if together:
                outs[k][i * depth : (i + 1) * depth, :] = value.astype(outs[k].dtype)
            else:
                outs[k][...] = value.astype(outs[k].dtype)
        if not together:
            outs = outs[count:]


def fold(chains, counts, me, together):
    width = chains[0][0].shape[1]
    depths = [chain[0].shape[0] // count for chain, count in zip(chains, counts)]
    if all(depth % 16 == 0 for depth in depths):
        groups = [(sum(depths), counts[0])] if together else list(zip(depths, counts))
        shapes = [
            jax.ShapeDtypeStruct((depth, width), BF16 if k else F32)
            for depth, count in groups
            for k in range(count)
        ]
        out = iter(kernel_call(
            functools.partial(
                fold_body, terms=[len(c) for c in chains], counts=counts, together=together
            ),
            shapes,
            smem=1,
        )(jnp.stack(me), *[term for chain in chains for term in chain]))
        return [[next(out) for _ in range(count)] for _, count in groups]
    found = []
    for chain, count, depth, at in zip(chains, counts, depths, me):
        parts = [
            total([lax.dynamic_slice_in_dim(t, (at ^ k) * depth, depth, 0) for t in chain])
            for k in range(count)
        ]
        found.append([part.astype(BF16) if k else part for k, part in enumerate(parts)])
    return [[jnp.concatenate(pair, 0) for pair in zip(*found)]] if together else found


def finish_body(core_ref, *refs, cuts):
    (p, p_far, q, q_far), outs, held, sems = refs[:4], refs[4:8], refs[8:12], refs[12]
    quarter = p.shape[0]
    for near_core in range(2):

        @pl.when(core_ref[0] == near_core)
        def _():
            order = [(p, p_far), (q, q_far)]
            order = [pair[core != near_core] for core in range(2) for pair in order]
            for i, (first, last) in enumerate(cuts):
                at = first
                while at < last:
                    number, place = at // quarter, at % quarter
                    upto = min(last, (number + 1) * quarter)
                    held[i][at - first : upto - first, :] = order[number][
                        place : place + upto - at, :
                    ].astype(F32)
                    at = upto
                pltpu.make_async_copy(held[i], outs[i], sems.at[i]).start()

    for i in range(len(cuts)):
        pltpu.make_async_copy(held[i], outs[i], sems.at[i]).wait()


class Slice:
    def __init__(self):
        self.groups, self.members = lax.axis_size("group"), lax.axis_size("member")
        self.size = {"c": 2, "y": self.groups // 2, "z": 4, "x": self.members // 4}
        group, member = lax.axis_index("group"), lax.axis_index("member")
        self.at = {
            "c": group % 2,
            "y": group // 2,
            "z": member // self.size["x"],
            "x": member % self.size["x"],
        }

    def swap(self, array, axis, k):
        stride = {"c": 1, "y": 2, "z": self.size["x"], "x": 1}[axis]
        name, count = ("group", self.groups) if axis in "cy" else ("member", self.members)
        return lax.ppermute(array, name, [(i, i ^ (k * stride)) for i in range(count)])

    def scatter(self, chains, axes, together=False):
        out = fold(chains, [self.size[a] for a in axes], [self.at[a] for a in axes], together)
        if together:
            axes = axes[:1]
        return [
            [mine] + [self.swap(part, axis, k + 1) for k, part in enumerate(parts)]
            for (mine, *parts), axis in zip(out, axes)
        ]

    def gather(self, part, axis, dtype=BF16, parts=1):
        pieces = [part] + [self.swap(part, axis, k) for k in range(1, self.size[axis])]
        return join(pieces, self.at[axis], dtype, parts)


def total(terms):
    out = terms[0].astype(F32)
    for term in terms[1:]:
        out = out + term.astype(F32)
    return out


def on_device(
    store,
    cache,
    hot_local,
    hit_member,
    hit_row,
    miss_owner,
    miss_row,
    tgt_self,
    tgt_nbr,
    tgt_mask,
    seed_self,
    seed_nbr,
    seed_mask,
    w1_self,
    w1_nbr,
    w2_self,
    w2_nbr,
    d_emb,
):
    box = Slice()
    nx, ny, nz = box.size["x"], box.size["y"], box.size["z"]
    wide, hid = w1_self.shape
    owners = box.groups * box.members
    hits, misses = hit_row.shape[0], miss_row.shape[0]
    cap = 2 * misses // owners
    seeds, fan_two = seed_nbr.shape
    rows = seeds * (fan_two + 1)

    share = cache.shape[0] // box.groups
    group = lax.axis_index("group")

    def cast_share(number):
        return lax.dynamic_slice_in_dim(cache, number * share, share, 0).astype(BF16)

    mine = cast_share(group)

    ids, slot = kernel_call(
        request_body,
        (
            jax.ShapeDtypeStruct((owners, cap), I32),
            jax.ShapeDtypeStruct((1, misses), I32),
        ),
    )(miss_owner.reshape(1, -1), miss_row.reshape(1, -1))
    store_low = store.astype(BF16)
    asked = lax.all_to_all(
        ids.reshape(owners, 1, cap), BOTH, split_axis=0, concat_axis=0, tiled=True
    ).reshape(owners, cap)
    near = [box.swap(mine, "z", k) for k in range(1, nz // 2)]

    targets = jnp.concatenate([seed_self[None, :], seed_nbr.T], 0)
    names = jnp.concatenate([tgt_self[None, :] + 1, jnp.where(tgt_mask > 0, tgt_nbr + 1, 0).T], 0)
    member, line = hit_member.reshape(1, -1), hit_row.reshape(1, -1)
    holder = line // share
    code = ((holder % 2) ^ box.at["c"]) * ny + ((holder // 2) ^ box.at["y"])
    code = code * nx + ((member % nx) ^ box.at["x"])
    code = code * nz + ((member // nx) ^ box.at["z"])
    code = code * share + line % share
    hot = lax.dynamic_slice_in_dim(store, hot_local[0, 0] * BLOCK, BLOCK, 0).astype(BF16)

    def side(part):
        found = {(k, 0): box.swap(part, "x", k) for k in range(1, nx)}
        return found | {(0, k): box.swap(part, "y", k) for k in range(1, ny)}

    def corner(sides, way=0):
        found = {}
        for i in range(1, nx):
            for j in range(1, ny):
                if way:
                    found[i, j] = [box.swap(sides[i, 0], "y", j) if way == 1 else box.swap(sides[0, j], "x", i)]
                    continue
                upper, lower = jnp.split(sides[i, 0], 2)[0], jnp.split(sides[0, j], 2)[1]
                found[i, j] = [box.swap(upper, "y", j), box.swap(lower, "x", i)]
        return found

    def cached(*batches):
        pieces, bases = [], []
        for first, batch in batches:
            for (i, j), held in batch.items():
                start = first
                for piece in held if isinstance(held, list) else [held]:
                    for k in range(2):
                        pieces.append(piece if k == 0 else box.swap(piece, "c", 1))
                        bases.append(((k * ny + j) * nx + i) * nz * share + start)
                    start += piece.shape[0]
        return kernel_call(
            functools.partial(cached_body, bases=bases),
            jax.ShapeDtypeStruct((hits, wide), BF16),
        )(code, *pieces)

    far = [box.swap(mine, "z", k) for k in range(nz // 2, nz - 1)]
    home = {(0, k): cast_share(group ^ (2 * k)) for k in range(1, ny)}
    home[0, 0] = mine
    beside = {(i, k): box.swap(home[0, k], "x", i) for i in range(1, nx) for k in range(ny)}
    near, last = lax.optimization_barrier((near, mine))
    near_own = near[0] if len(near) == 1 else jnp.concatenate(near, 0)
    half = share + near_own.shape[0]
    near_side = side(near_own)
    far.append(box.swap(last, "z", nz - 1))
    asked, store_low, near_side, beside = lax.optimization_barrier(
        (asked, store_low, near_side, beside)
    )
    served = kernel_call(
        serve_body,
        jax.ShapeDtypeStruct((owners * cap, wide), BF16),
    )(asked, store_low)
    near_corner = corner(near_side, 1)
    served, far, hot, names = lax.optimization_barrier((served, far, hot, names))
    miss_rows = lax.all_to_all(
        served.reshape(owners, cap, wide), BOTH, split_axis=0, concat_axis=0, tiled=True
    ).reshape(owners * cap, wide)

    sel_hit, sel_miss, count, back, flags, code = kernel_call(
        functools.partial(tables_body, hits=hits),
        (
            jax.ShapeDtypeStruct((2, rows, hits), BF16),
            jax.ShapeDtypeStruct((2, rows, owners * cap), BF16),
            jax.ShapeDtypeStruct((rows, 1), F32),
            jax.ShapeDtypeStruct((rows, hid), BF16),
            jax.ShapeDtypeStruct((seeds, fan_two), F32),
            jax.ShapeDtypeStruct((hits, 1), I32),
        ),
    )(targets, names, slot, seed_mask.T, code, d_emb, w2_self, w2_nbr)

    far_own = jnp.concatenate(far, 0)
    far_side = side(far_own)
    first = cached((0, home), (share, {(0, 0): near_own}), (half, {(0, 0): far_own}))
    second = cached((0, beside), (share, near_side))
    far_side, near_corner, first, second = lax.optimization_barrier(
        (far_side, near_corner, first, second)
    )
    far_corner = corner(far_side)
    third = cached((half, far_side))
    far_corner, third = lax.optimization_barrier((far_corner, third))
    fourth = cached((share, near_corner), (half, far_corner))
    own_part, near_part = kernel_call(
        share_body,
        (
            jax.ShapeDtypeStruct((rows, wide), BF16),
            jax.ShapeDtypeStruct((rows, wide), F32),
        ),
    )(sel_hit, first, second, third, fourth)

    hot, own_part, near_part = lax.optimization_barrier((hot, own_part, near_part))
    far_hot = [hot] + [box.swap(hot, "y", k) for k in range(1, ny)]
    grad_scale = 1.0 / math.sqrt(seeds * owners)
    total_rows = 2 * wide + 2 * hid
    vmem, hbm = pl.BlockSpec(memory_space=pltpu.VMEM), pl.BlockSpec(memory_space=pltpu.HBM)
    streamed = (
        miss_rows, w1_self, w1_nbr, back, w2_self, w2_nbr, d_emb, sel_miss, own_part, near_part
    )
    turn = 384
    emb, *sums = pl.pallas_call(
        functools.partial(step_body, scale=grad_scale, step=turn),
        out_shape=(
            jax.ShapeDtypeStruct((seeds, hid), BF16),
            *[jax.ShapeDtypeStruct((total_rows // 4, hid), kind) for kind in (BF16,) * 4],
        ),
        in_specs=[pl.BlockSpec(memory_space=pltpu.SMEM)] + [hbm] * 10 + [vmem] * 2,
        out_specs=(vmem,) * 5,
        scratch_shapes=[pltpu.VMEM(array.shape, array.dtype) for array in streamed]
        + [
            pltpu.VMEM((rows, wide), BF16),
            pltpu.VMEM((rows, wide), BF16),
            pltpu.VMEM((rows, hid), BF16),
            pltpu.VMEM((rows, hid), BF16),
            pltpu.SemaphoreType.DMA((7 + 3 * (rows // turn),)),
        ],
        compiler_params=pltpu.CompilerParams(vmem_limit_bytes=2 * GRANT),
        cost_estimate=pl.CostEstimate(
            flops=0, bytes_accessed=0, transcendentals=0
        ),
    )(box.at["c"].reshape(1), *streamed, count, flags)
    sums, far_hot = lax.optimization_barrier((sums, far_hot))

    p, q = ([sums[2 + i].astype(F32), box.swap(sums[i], "c", 1)] for i in range(2))
    p, q = box.scatter((p, q), ("x", "y"))
    near_hot = [box.swap(block, "c", 1) for block in far_hot]
    p, q, near_hot = lax.optimization_barrier((p, q, near_hot))
    pairs = [join(pair, box.at["c"], BF16)[0] for pair in zip(far_hot, near_hot)]
    (new_cache,) = join(pairs, box.at["y"], F32)
    p, q = box.scatter((p, q), ("y", "x"))
    (summed,) = box.scatter((p, q), ("z", "z"), together=True)
    summed = total(summed).astype(BF16)
    p, q = box.gather(summed, "z", parts=2)
    (p,), (q,) = lax.optimization_barrier((box.gather(p, "y"), box.gather(q, "x")))
    (p,), (q,) = box.gather(p, "x"), box.gather(q, "y")
    p, q = (p, box.swap(p, "c", 1)), (q, box.swap(q, "c", 1))
    cuts = [(0, wide), (wide, 2 * wide), (2 * wide, 2 * wide + hid), (2 * wide + hid, total_rows)]
    shapes = [jax.ShapeDtypeStruct((last - at, hid), F32) for at, last in cuts]
    grads = pl.pallas_call(
        functools.partial(finish_body, cuts=cuts),
        out_shape=shapes,
        in_specs=[pl.BlockSpec(memory_space=pltpu.SMEM)] + [vmem] * 4,
        out_specs=[hbm] * 4,
        scratch_shapes=[pltpu.VMEM(x.shape, x.dtype) for x in shapes]
        + [pltpu.SemaphoreType.DMA((4,))],
        compiler_params=pltpu.CompilerParams(vmem_limit_bytes=GRANT),
    )(box.at["c"].reshape(1), *p, *q)
    return (emb, *grads, new_cache)


def solution(mesh):
    split = P(BOTH)
    in_specs = (split, P("member")) + (split,) * 11 + (P(),) * 4 + (split,)
    out_specs = (split, P(), P(), P(), P(), P("member"))
    return jax.shard_map(
        on_device, mesh=mesh, in_specs=in_specs, out_specs=out_specs, check_vma=False
    )
```
